128 devices in a mesh: tm: 64 (over z, y, x), blk: 2 (over core).
Axes of the slice: x: 4, y: 4, z: 4, core: 2. Of those that a mesh axis runs over, the one named last changes fastest.
Arguments:
- spatial_factor: bfloat16 [49152, 768], P(('tm', 'blk')), may hold values from -1 to 2
- transition_factor: bfloat16 [49152, 768], P(('tm', 'blk')), may hold values from -3 to 1
- effect_factor: bfloat16 [4096, 768], P(('tm', 'blk')), may hold values from -0.21875 to 0.21875
- node_diag: float32 [49152], P(('tm', 'blk')), may hold values from 0.05 to 0.5
Outputs:
- ends_sys: float32 [64, 2, 768, 1536], P('tm', None, 'blk')
- arrow_sys: float32 [64, 64, 1600], P('tm', 'blk')
- logpivot: float32 [64], P('tm')
The draws below stay inside these ranges and needn't reach their ends.
All inputs are finite; a program needn't handle non-finite values.
Results may differ from the reference program's by a relative error of at most 0.0003.
Values may be sent and summed in bfloat16 or wider, within the bound.
No kernel may reach another device: no remote copies, remote signals or barrier semaphores. Data moves between devices by JAX's collectives and lax.ppermute only.
A program may use at most 128 MiB of HBM per device.

```python
import math
import jax
import jax.numpy as jnp
from jax import lax

NODES = 768
FIXED = 64
LEVELS = 3
TSTEPS = 64
GROUP = 8


def spatial_blocks(key, spread):
    first_key = jax.random.fold_in(key, 0)
    third_key = jax.random.fold_in(key, 2)
    bell = jnp.clip(jax.random.normal(first_key, (TSTEPS, NODES, NODES), jnp.float32), -4.0, 4.0)
    noise = bell * (spread / math.sqrt(NODES))
    levels = jax.random.uniform(third_key, (TSTEPS, NODES), jnp.float32, 1.0, 2.0)
    unit = jnp.eye(NODES, dtype=jnp.float32)
    return noise * (1.0 - unit)[None] + levels[:, :, None] * unit[None]


def draw_spatial_factor(key, part):
    blocks = spatial_blocks(key, 0.75)
    return blocks.reshape(TSTEPS * NODES, NODES).astype(jnp.bfloat16)


def draw_transition_factor(key, part):
    blocks = spatial_blocks(key, 0.75)
    key = jax.random.fold_in(key, 2)
    jitter = jnp.clip(jax.random.normal(key, (TSTEPS, NODES, NODES), jnp.float32), -4.0, 4.0) * (0.15 / math.sqrt(NODES))
    following = jnp.roll(blocks, -1, axis=0)
    return (jitter - following).reshape(TSTEPS * NODES, NODES).astype(jnp.bfloat16)


def block_scale(stream_key, extent, cuts, least, top_value):
    level = 1.0
    for axis_at, parts in cuts:
        steps = jax.random.uniform(jax.random.fold_in(jax.random.fold_in(stream_key, 6), axis_at), (parts,), jnp.float32, least / len(cuts), top_value / len(cuts))
        level = level * jnp.repeat(jnp.exp(steps), extent[axis_at] // parts).reshape((-1,) + (1,) * (len(extent) - 1 - axis_at))
    return level


def centred(own_key, extent, width, limit, cuts=(), held_as=jnp.bfloat16):
    array = width * jax.random.normal(own_key, extent, jnp.float32)
    if cuts:
        array = array * block_scale(own_key, extent, cuts, -0.22, 0.18)
    return jnp.clip(array, -limit, limit).astype(held_as)


def setup_inputs(seed: int = 0) -> dict:
    key_list = jax.random.split(jax.random.key(seed), 5)
    return {
        "spatial_factor": draw_spatial_factor(jax.random.fold_in(key_list[4], 71), 0),
        "transition_factor": draw_transition_factor(jax.random.fold_in(key_list[4], 71), 0),
        "effect_factor": centred(key_list[2], (TSTEPS * FIXED, NODES), NODES ** -0.5, 0.21875, ((0, 128),)),
        "node_diag": jnp.clip(jnp.exp(math.log(0.5) - 2.3025851 * jax.random.uniform(key_list[3], (TSTEPS * NODES,), jnp.float32) ** block_scale(key_list[3], (TSTEPS * NODES,), ((0, 128),), -0.2, 0.2)), 0.05, 0.5),
    }


def leaf_system(spatial_block, transition_block, effect_block, diag_block):
    stacked = jnp.concatenate([spatial_block, transition_block, effect_block], axis=0)
    system = jnp.dot(stacked.astype(jnp.float32), stacked.T.astype(jnp.float32), preferred_element_type=jnp.float32)
    padding = jnp.zeros((stacked.shape[0] - diag_block.shape[0],), jnp.float32)
    return system + jnp.diag(jnp.concatenate([diag_block, padding]))

def join_segments(lower_seg, upper_seg):
    first = slice(0, NODES)
    after = slice(NODES, 2 * NODES)
    effects = slice(2 * NODES, None)
    pivot = lower_seg[after, after] + upper_seg[first, first]
    pivot_chol = jnp.linalg.cholesky(pivot)
    coupling = jnp.concatenate([lower_seg[after, first], upper_seg[first, after], lower_seg[after, effects] + upper_seg[first, effects]], axis=1)
    solved = jax.scipy.linalg.solve_triangular(pivot_chol, coupling, lower=True)
    blank = jnp.zeros((NODES, NODES), jnp.float32)
    row_first = jnp.concatenate([lower_seg[first, first], blank, lower_seg[first, effects]], axis=1)
    row_after = jnp.concatenate([blank, upper_seg[after, after], upper_seg[after, effects]], axis=1)
    row_effects = jnp.concatenate([lower_seg[effects, first], upper_seg[effects, after], lower_seg[effects, effects] + upper_seg[effects, effects]], axis=1)
    retained = jnp.concatenate([row_first, row_after, row_effects], axis=0)
    correction = jnp.dot(solved.T.astype(jnp.float32), solved.astype(jnp.float32), precision=lax.Precision.HIGHEST, preferred_element_type=jnp.float32)
    step_logs = 2.0 * jnp.sum(jnp.log(jnp.diag(pivot_chol)))
    return (retained - correction, step_logs)

def reduce_group(pieces):
    spatial_group, transition_group, effect_group, diag_group = pieces
    systems = [leaf_system(spatial_group[member], transition_group[member], effect_group[member], diag_group[member]) for member in range(GROUP)]
    logs = [jnp.zeros((), jnp.float32) for member in range(GROUP)]
    for level_index in range(LEVELS):
        new_systems = []
        new_logs = []
        for pair_index in range(len(systems) // 2):
            joined, step_logs = join_segments(systems[2 * pair_index], systems[2 * pair_index + 1])
            new_systems.append(joined)
            new_logs.append(logs[2 * pair_index] + logs[2 * pair_index + 1] + step_logs)
        systems = new_systems
        logs = new_logs
    return (systems[0], logs[0])

def reference(spatial_factor, transition_factor, effect_factor, node_diag):
    groups = TSTEPS // GROUP
    spatial_group = spatial_factor.reshape(groups, GROUP, NODES, NODES)
    transition_group = transition_factor.reshape(groups, GROUP, NODES, NODES)
    effect_group = effect_factor.reshape(groups, GROUP, FIXED, NODES)
    diag_group = node_diag.reshape(groups, GROUP, NODES)
    systems, logs = lax.map(reduce_group, (spatial_group, transition_group, effect_group, diag_group))
    flipped = jnp.swapaxes(systems, 1, 2)
    ends = flipped[:, :2 * NODES, :2 * NODES].reshape(groups, 2, NODES, 2 * NODES)
    arrow = flipped[:, 2 * NODES:, :]
    ends_sys = jnp.repeat(ends, GROUP, axis=0)
    arrow_sys = jnp.repeat(arrow, GROUP, axis=0)
    logpivot = jnp.repeat(logs / ((GROUP - 1) * NODES), GROUP)
    return (ends_sys, arrow_sys, logpivot)
```

```python
import functools

import jax
import jax.numpy as jnp
from jax import lax
from jax.experimental import pallas as pl
from jax.experimental.pallas import tpu as pltpu
from jax.sharding import PartitionSpec as P

F32 = jnp.float32
BF16 = jnp.bfloat16
TILE = 8
LANES = 128


def split(x):
    high = x.astype(BF16)
    return high, (x - high.astype(F32)).astype(BF16)


def dot3(a, b):
    dot = functools.partial(jnp.dot, preferred_element_type=F32)
    return dot(a[0], b[0]) + (dot(a[0], b[1]) + dot(a[1], b[0]))


def rows8(v, q):
    return jnp.broadcast_to(v[q : q + 1, :], (TILE, LANES))


def lane8(v, j):
    return jnp.broadcast_to(v[:, j : j + 1], (TILE, LANES))


def invert8(cols):
    sub = lax.broadcasted_iota(jnp.int32, (TILE, LANES), 0)
    pivots = []
    for q in range(TILE):
        here = sub == q
        row = [rows8(cols[j], q) for j in range(TILE)]
        pivots.append(row[q][0:1])
        inv = pltpu.reciprocal(row[q], approx=True)
        inv = inv * (2.0 - row[q] * inv)
        new = []
        for j in range(TILE):
            if j == q:
                new.append(jnp.where(here, inv, -cols[q] * inv))
            else:
                scaled = row[j] * inv
                new.append(jnp.where(here, scaled, cols[j] - cols[q] * scaled))
        cols = new
    return cols, pivots


def invert128(tiles):
    lane = lax.broadcasted_iota(jnp.int32, (TILE, LANES), 1)
    sub = lax.broadcasted_iota(jnp.int32, (TILE, LANES), 0)
    logs = jnp.zeros((1, LANES), F32)
    for p in range(LANES // TILE):
        inside = (lane >= TILE * p) & (lane < TILE * p + TILE)
        own = tiles[p]
        inverse, pivots = invert8([lane8(own, TILE * p + j) for j in range(TILE)])
        for pivot in pivots:
            logs = logs + jnp.log(pivot)
        own = jnp.where(inside, (lane - TILE * p == sub).astype(F32), own)
        parts = [inverse[j] * rows8(own, j) for j in range(TILE)]
        solved = ((parts[0] + parts[1]) + (parts[2] + parts[3])) + (
            (parts[4] + parts[5]) + (parts[6] + parts[7])
        )
        spread = [rows8(solved, j) for j in range(TILE)]
        new = []
        for i in range(LANES // TILE):
            if i == p:
                new.append(solved)
                continue
            parts = [lane8(tiles[i], TILE * p + j) * spread[j] for j in range(TILE)]
            total = ((parts[0] + parts[1]) + (parts[2] + parts[3])) + (
                (parts[4] + parts[5]) + (parts[6] + parts[7])
            )
            new.append(jnp.where(inside, 0.0, tiles[i]) - total)
        tiles = new
    return tiles, logs


def inverse_kernel(m_ref, o_ref, l_ref):
    size = m_ref.shape[0]
    o_ref[...] = m_ref[...]

    def body(k, logs):
        ks = pl.ds(pl.multiple_of(k * LANES, LANES), LANES)
        tiles = [
            o_ref[pl.ds(pl.multiple_of(k * LANES + TILE * i, TILE), TILE), ks]
            for i in range(LANES // TILE)
        ]
        tiles, more = invert128(tiles)
        block = jnp.concatenate(tiles, 0)
        block_parts = split(block)
        col = split(o_ref[:, ks])
        solved = dot3(block_parts, split(o_ref[ks, :]))
        update = dot3(col, split(solved))
        left = dot3(col, block_parts)
        o_ref[...] = o_ref[...] - update
        o_ref[:, ks] = -left
        o_ref[ks, :] = solved
        o_ref[ks, ks] = block
        return logs + more

    logs = lax.fori_loop(0, size // LANES, body, jnp.zeros((1, LANES), F32))
    l_ref[...] = jnp.broadcast_to(logs, (TILE, LANES))


def inverse(m):
    size = m.shape[0]
    vmem = pl.BlockSpec(memory_space=pltpu.VMEM)
    return pl.pallas_call(
        inverse_kernel,
        out_shape=(
            jax.ShapeDtypeStruct((size, size), F32),
            jax.ShapeDtypeStruct((TILE, LANES), F32),
        ),
        in_specs=[vmem],
        out_specs=(vmem, vmem),
        compiler_params=pltpu.CompilerParams(vmem_limit_bytes=40 << 20),
        cost_estimate=pl.CostEstimate(
            flops=30_000_000_000, bytes_accessed=8 * size * size, transcendentals=size
        ),
        name="inverse",
    )(m)


def high(a, b):
    return lax.dot_general(
        a,
        b,
        (((0,), (0,)), ((), ())),
        precision=lax.Precision.HIGH,
        preferred_element_type=F32,
    )


def outer(a, b):
    return lax.dot_general(a, b, (((1,), (1,)), ((), ())), preferred_element_type=F32)


def shards(spatial, transition, effect, diag):
    half = spatial.shape[0]
    nodes = 2 * half
    steps = lax.axis_size("tm")
    index = lax.axis_index("tm")
    core = lax.axis_index("blk")
    bit = [(index // 2**r) % 2 for r in range(3)]

    def other_core(x):
        return lax.ppermute(x, "blk", [(0, 1), (1, 0)])

    def partner(x, level):
        if level == 1:
            pairs = [(t, (t // 4) * 4 + 3 - t % 4) for t in range(steps)]
        else:
            pairs = [(t, t ^ (1, 2, 4)[level]) for t in range(steps)]
        return lax.ppermute(x, "tm", pairs)

    def both(x):
        return jnp.concatenate([x, other_core(x)], axis=0)

    def turned(x):
        mid = x.shape[0] // 2
        return jnp.concatenate([x[mid:], x[:mid]], axis=0)

    def join(inv, x1, x2, xk, w1, w2, wk1, wk2, wkk, last):
        own = jnp.concatenate([x1, x2, xk], axis=1)
        far = turned(other_core(own))
        c1, c2, ck = high(inv, x1), high(inv, x2), high(inv, xk)
        f1 = jnp.concatenate([x1, far[:, :half]], axis=1)
        f2 = jnp.concatenate([x2, far[:, half:nodes]], axis=1)
        fk = jnp.concatenate([xk, far[:, nodes:]], axis=1)
        if last:
            flip = core == 1
            f1 = jnp.where(flip, jnp.concatenate([far[:, :half], x1], axis=1), f1)
            f2 = jnp.where(flip, jnp.concatenate([far[:, half:nodes], x2], axis=1), f2)
            fk = jnp.where(flip, jnp.concatenate([far[:, nodes:], xk], axis=1), fk)
            w1, w2, wk1, wk2, wkk = [
                jnp.where(flip, turned(w), w).T for w in (w1, w2, wk1, wk2, wkk)
            ]
            return (
                jnp.concatenate([w1 - high(c1, f1), -high(c1, f2)], axis=1),
                jnp.concatenate([-high(c2, f1), w2 - high(c2, f2)], axis=1),
                jnp.concatenate(
                    [wk1 - high(ck, f1), wk2 - high(ck, f2), wkk - high(ck, fk)], axis=1
                ),
            )
        return (
            w1 - high(f1, c1),
            -high(f1, c2),
            wk1 - high(f1, ck),
            w2 - high(f2, c2),
            wk2 - high(f2, ck),
            wkk - high(fk, ck),
        )

    lower = bit[0] == 0
    pivot_own = jnp.where(lower, transition, spatial)
    keep_own = jnp.where(lower, spatial, transition)
    pivot_got = partner(pivot_own, 0)
    diag_got = partner(diag, 0)
    keep_got = partner(keep_own, 0)
    effect_got = partner(effect, 0)
    p_own, p_got = both(pivot_own), both(pivot_got)
    pivot_diag = both(jnp.where(lower, diag_got, diag))
    stacked = jnp.concatenate([p_own, p_got], axis=1)
    ids = lax.broadcasted_iota(jnp.int32, (nodes, nodes), 0)
    eye = ids == lax.broadcasted_iota(jnp.int32, (nodes, nodes), 1)
    m = outer(stacked, stacked) + jnp.where(eye, pivot_diag[None, :], 0.0)
    inv, logs = inverse(m)
    mine = bit[0] != bit[1]
    p1, p2 = jnp.where(mine, p_own, p_got), jnp.where(mine, p_got, p_own)
    k1, k2 = jnp.where(mine, keep_own, keep_got), jnp.where(mine, keep_got, keep_own)
    e1, e2 = jnp.where(mine, effect, effect_got), jnp.where(mine, effect_got, effect)
    keep_diag = jnp.where(lower, diag, diag_got)
    after = bit[1] == 1
    s1, s2 = both(k1), both(k2)
    eye_half = eye[:, :half]
    w1 = outer(s1, k1) + jnp.where(eye_half & after, keep_diag[None, :], 0.0)
    w2 = outer(s2, k2) + jnp.where(eye_half & ~after, keep_diag[None, :], 0.0)
    ef1, ef2 = both(e1), both(e2)
    ee, er, ek, rr, rk, kk = join(
        inv,
        outer(p1, k1),
        outer(p2, k2),
        outer(p1, e1) + outer(p2, e2),
        w1,
        w2,
        outer(s1, e1),
        outer(s2, e2),
        outer(ef1, e1) + outer(ef2, e2),
        False,
    )
    total = jnp.sum(logs[0:1, 0:1])
    for level in (1, 2):
        last = level == 2
        m_own = ee + partner(ee, level)
        coupling = jnp.concatenate([er, ek], axis=1)
        coupling_got = partner(coupling, level)
        rr_got = partner(rr, level)
        small = jnp.concatenate([rk, kk], axis=0)
        small_got = partner(small, level)
        total_got = partner(total, level)
        m = jnp.concatenate([m_own, turned(other_core(m_own))], axis=1)
        inv, logs = inverse(m)
        mine = bit[2] == 0 if last else bit[1] != bit[2]
        er_got, ek_got = coupling_got[:, :half], coupling_got[:, half:]
        rk_got, kk_got = small_got[:nodes], small_got[nodes:]
        result = join(
            inv,
            jnp.where(mine, er, er_got),
            jnp.where(mine, er_got, er),
            ek + ek_got,
            jnp.where(mine, rr, rr_got),
            jnp.where(mine, rr_got, rr),
            jnp.where(mine, rk, rk_got),
            jnp.where(mine, rk_got, rk),
            kk + kk_got,
            last,
        )
        total = total + total_got + jnp.sum(logs[0:1, 0:1])
        if not last:
            ee, er, ek, rr, rk, kk = result
    ends = jnp.stack([result[0], result[1]], axis=0)[None]
    return ends, result[2][None], (total / (7 * nodes)).reshape(1)


def solution(mesh):
    return jax.shard_map(
        shards,
        mesh=mesh,
        in_specs=(
            P(("tm", "blk"), None),
            P(("tm", "blk"), None),
            P(("tm", "blk"), None),
            P(("tm", "blk")),
        ),
        out_specs=(P("tm", None, "blk", None), P("tm", "blk", None), P("tm")),
        check_vma=False,
    )
```

```python
import functools

import jax
import jax.numpy as jnp
from jax import lax
from jax.experimental import pallas as pl
from jax.experimental.pallas import tpu as pltpu
from jax.sharding import PartitionSpec as P

F32 = jnp.float32
BF16 = jnp.bfloat16
TILE = 8
LANES = 128


def split(x):
    high = x.astype(BF16)
    return high, (x - high.astype(F32)).astype(BF16)


def nn(a, b):
    return jnp.dot(a, b, preferred_element_type=F32)


def dot3(a, b):
    return nn(a[0], b[0]) + (nn(a[0], b[1]) + nn(a[1], b[0]))


def rows8(v, q):
    return jnp.broadcast_to(v[q : q + 1, :], (TILE, LANES))


def lane8(v, j):
    return jnp.broadcast_to(v[:, j : j + 1], (TILE, LANES))


SUBS = 2 * TILE


def solve16(own, p, lane, sub):
    at = SUBS * p
    inside = (lane >= at) & (lane < at + SUBS)
    cols = [[lane8(own[t], at + j) for t in range(2)] for j in range(SUBS)]
    cur = [jnp.where(inside, (lane - at - TILE * t == sub).astype(F32), own[t]) for t in range(2)]
    dets = []
    for q in range(0, SUBS, 2):
        tq, sq = q // TILE, q % TILE
        first, second = sub == sq, sub == sq + 1
        either = first | second
        a, b = rows8(cols[q][tq], sq), rows8(cols[q + 1][tq], sq)
        d, c = rows8(cols[q][tq], sq + 1), rows8(cols[q + 1][tq], sq + 1)
        det = a * c - b * d
        dets.append(det[0:1])
        inv = pltpu.reciprocal(det, approx=True)
        f, g = list(cols[q]), list(cols[q + 1])
        f[tq] = jnp.where(first, -1.0, jnp.where(second, 0.0, f[tq]))
        g[tq] = jnp.where(second, -1.0, jnp.where(first, 0.0, g[tq]))

        def apply(v):
            x, y = rows8(v[tq], sq), rows8(v[tq], sq + 1)
            u, w = c * x - b * y, a * y - d * x
            base = [jnp.where(either, 0.0, v[t]) if t == tq else v[t] for t in range(2)]
            return [base[t] - (f[t] * u + g[t] * w) * inv for t in range(2)]

        for j in range(q + 2, SUBS):
            cols[j] = apply(cols[j])
        cur = apply(cur)
    return cur, dets, inside


def invert128(tiles):
    lane = lax.broadcasted_iota(jnp.int32, (TILE, LANES), 1)
    sub = lax.broadcasted_iota(jnp.int32, (TILE, LANES), 0)
    logs = jnp.zeros((1, LANES), F32)
    width = 2 * SUBS
    for g in range(LANES // width):
        panel = list(tiles[4 * g : 4 * g + 4])
        for s in range(2):
            p = 2 * g + s
            cur, dets, inside = solve16(panel[2 * s : 2 * s + 2], p, lane, sub)
            for det in dets:
                logs = logs + jnp.log(det)
            spread = [rows8(cur[m // TILE], m % TILE) for m in range(SUBS)]
            new = list(panel)
            for i in range(4):
                if i // 2 == s:
                    new[i] = cur[i % 2]
                    continue
                parts = [lane8(panel[i], SUBS * p + m) * spread[m] for m in range(SUBS)]
                while len(parts) > 1:
                    parts = [parts[m] + parts[m + 1] for m in range(0, len(parts), 2)]
                new[i] = jnp.where(inside, 0.0, panel[i]) - parts[0]
            panel = new
        high, low = split(jnp.concatenate(panel, 0))
        left = split(jnp.concatenate(tiles, 0))

        def padded(v):
            parts = [v]
            if g:
                parts.insert(0, jnp.zeros((width * g, LANES), BF16))
            if width * (g + 1) < LANES:
                parts.append(jnp.zeros((LANES - width * (g + 1), LANES), BF16))
            return jnp.concatenate(parts, 0)

        right = padded(high)
        update = nn(jnp.concatenate(left, 1), jnp.concatenate([right, right], 0))
        update = update + nn(left[0], padded(low))
        inside = (lane >= width * g) & (lane < width * (g + 1))
        tiles = [
            panel[i - 4 * g]
            if 4 * g <= i < 4 * g + 4
            else jnp.where(inside, 0.0, tiles[i]) - update[TILE * i : TILE * i + TILE]
            for i in range(LANES // TILE)
        ]
    return tiles, logs


HALF = 384
NODES = 2 * HALF
FIX = 32
PARTS = HALF // LANES


def nt(a, b):
    return lax.dot_general(a, b, (((1,), (1,)), ((), ())), preferred_element_type=F32)


def nt3(a, b):
    return nt(a[0], b[0]) + (nt(a[0], b[1]) + nt(a[1], b[0]))


def diag_slot(r, s):
    return r * (r + 1) // 2 + s


def off_slot(r, s):
    return 6 + s * (s + 1) // 2 + r


def blk(r):
    return slice(r * LANES, r * LANES + LANES)


def pack(dst, value):
    for r in range(PARTS):
        for s in range(PARTS):
            if r >= s:
                dst[diag_slot(r, s)] = value[blk(r), blk(s)]
            if r <= s:
                dst[off_slot(r, s)] = value[blk(r), HALF + s * LANES : HALF + (s + 1) * LANES]


def unpack_block(mine, theirs, r, s):
    if s < PARTS:
        return mine(diag_slot(r, s)) if r >= s else mine(diag_slot(s, r)).T
    s -= PARTS
    return mine(off_slot(r, s)) if r <= s else theirs(off_slot(s, r)).T


def eliminate(o_ref, hi_ref, lo_ref, l_ref, col, top, low, u_ref, d_ref):
    size = o_ref.shape[0]
    count = size // LANES
    col[...] = jnp.zeros(col.shape, BF16)
    top[...] = jnp.zeros(top.shape, BF16)
    low[...] = jnp.zeros(low.shape, BF16)
    u_ref[...] = o_ref[0:LANES, :]
    d_ref[...] = o_ref[0:LANES, 0:LANES]

    def late_update():
        for j in range(count):
            update = nn(col[...], top[:, blk(j)]) + nn(col[:, 0:LANES], low[:, blk(j)])
            o_ref[:, blk(j)] = o_ref[:, blk(j)] - update

    def at(k):
        return pl.ds(pl.multiple_of(k * LANES, LANES), LANES)

    def body(k, logs):
        ks, before, after = at(k), at(jnp.maximum(k - 1, 0)), at(jnp.minimum(k + 1, count - 1))
        late_update()
        tiles, more = invert128([d_ref[TILE * i : TILE * i + TILE, :] for i in range(LANES // TILE)])
        o_ref[before, :] = u_ref[...]
        block = jnp.concatenate(tiles, 0)
        parts = split(block)
        wide = jnp.concatenate(parts, 1)

        def solve(right):
            return nn(wide, jnp.concatenate([right[0], right[0]], 0)) + nn(parts[0], right[1])

        high, rest = split(o_ref[:, ks])
        col[:, 0:LANES] = high
        col[:, LANES : 2 * LANES] = rest
        ahead = split(solve(split(o_ref[ks, after])))
        left = col[after, :]
        update = nn(left, jnp.concatenate([ahead[0], ahead[0]], 0)) + nn(left[:, 0:LANES], ahead[1])
        d_ref[...] = o_ref[after, after] - update
        u_ref[...] = solve(split(o_ref[ks, :]))
        u_ref[:, ks] = block
        high, rest = split(u_ref[...])
        top[0:LANES, :] = high
        top[LANES : 2 * LANES, :] = high
        low[...] = rest
        o_ref[:, ks] = jnp.zeros((size, LANES), F32)
        return logs + more

    logs = lax.fori_loop(0, count, body, jnp.zeros((1, LANES), F32))
    late_update()
    o_ref[size - LANES : size, :] = u_ref[...]
    l_ref[...] = jnp.broadcast_to(logs, (TILE, LANES))
    for r in range(count):
        high, rest = split(o_ref[blk(r), :])
        hi_ref[blk(r), :] = high
        lo_ref[blk(r), :] = rest


def first_inverse_kernel(p_ref, q_ref, po_ref, qo_ref, d_ref, hi_ref, lo_ref, l_ref, m_ref, *more):
    *more, s_ref = more
    s_ref[:HALF, :NODES] = p_ref[...]
    s_ref[:HALF, NODES:] = q_ref[...]
    s_ref[HALF:, :NODES] = po_ref[...]
    s_ref[HALF:, NODES:] = qo_ref[...]
    eye = lax.broadcasted_iota(jnp.int32, (LANES, LANES), 0) == lax.broadcasted_iota(
        jnp.int32, (LANES, LANES), 1
    )
    for r in range(2 * PARTS):
        m_ref[blk(r), :] = nt(s_ref[blk(r), :], s_ref[...])
        m_ref[blk(r), blk(r)] += jnp.where(eye, d_ref[0:1, blk(r)], 0.0)
    eliminate(m_ref, hi_ref, lo_ref, l_ref, *more)


def next_inverse_kernel(p_ref, q_ref, po_ref, qo_ref, hi_ref, lo_ref, l_ref, m_ref, *more):
    mine = lambda i: p_ref[i] + q_ref[i]
    theirs = lambda i: po_ref[i] + qo_ref[i]
    for r in range(PARTS):
        for s in range(2 * PARTS):
            block = unpack_block(mine, theirs, r, s)
            m_ref[blk(r), blk(s)] = block
            if s >= PARTS:
                m_ref[blk(s), blk(r)] = block.T
        for s in range(r + 1):
            block = theirs(diag_slot(r, s))
            m_ref[blk(PARTS + r), blk(PARTS + s)] = block
            if s < r:
                m_ref[blk(PARTS + s), blk(PARTS + r)] = block.T
    eliminate(m_ref, hi_ref, lo_ref, l_ref, *more)


def pick(flag, dst, a, b):
    @pl.when(flag)
    def _():
        dst[...] = a[...]

    @pl.when(jnp.logical_not(flag))
    def _():
        dst[...] = b[...]


def put(xh, xl, at, value):
    rows = value.shape[0]
    high, low = split(value)
    xh[at : at + rows, :] = high
    xl[at : at + rows, :] = low


def turned(x):
    return jnp.concatenate([x[:, HALF:], x[:, :HALF]], axis=1)


def factors_in(flag, which, refs, oth_refs, dst):
    rows = refs[0].shape[0]
    a, b = refs if which == 0 else refs[::-1]
    pick(flag, dst.at[0:rows], a, b)
    a, b = oth_refs if which == 0 else oth_refs[::-1]
    pick(flag, dst.at[rows : 2 * rows], a, b)


CHUNK = 256


def solve_rows(xh, xl, at, rows, hi, lo, ch, cl):
    rs = slice(at, at + rows)
    for n in range(0, NODES, CHUNK):
        cs = slice(n, n + CHUNK)
        high, low = split(dot3((xh[rs, :], xl[rs, :]), (hi[:, cs], lo[:, cs])))
        ch[rs, cs] = high
        cl[rs, cs] = low


def products(ch, cl, at, rows, xh, xl, start, count):
    rs = slice(at, at + rows)
    for n in range(0, count, CHUNK):
        width = min(CHUNK, count - n)
        cs = slice(start + n, start + n + width)
        yield slice(n, n + width), nt3((ch[rs, :], cl[rs, :]), (xh[cs, :], xl[cs, :]))


def load_first_1(flag, f, xh, xl, w1, p, k):
    factors_in(flag, 0, (f["p"], f["q"]), (f["po"], f["qo"]), p)
    factors_in(flag, 0, (f["k"], f["j"]), (f["ko"], f["jo"]), k)
    for r in range(2 * PARTS):
        put(xh, xl, r * LANES, nt(k[blk(r), :], p[...]))
    first_w(f, 0, k, w1)


def first_w(f, which, k, w):
    eye = lax.broadcasted_iota(jnp.int32, (LANES, LANES), 0) == lax.broadcasted_iota(
        jnp.int32, (LANES, LANES), 1
    )
    for r in range(PARTS):
        w[blk(r), :] = nt(k[blk(r), :], k[...])
        w[blk(r), blk(r)] += jnp.where(eye, f["d"][which : which + 1, blk(r)], 0.0)


def load_first_2(flag, f, xh, xl, w2, wk, p, k, e, g):
    factors_in(flag, 0, (f["p"], f["q"]), (f["po"], f["qo"]), p)
    factors_in(flag, 0, (f["k"], f["j"]), (f["ko"], f["jo"]), k)
    factors_in(flag, 0, (f["e"], f["g"]), (f["eo"], f["go"]), e)
    factors_in(flag, 1, (f["e"], f["g"]), (f["eo"], f["go"]), g)
    for r in range(2 * PARTS):
        put(xh, xl, r * LANES, nt(k[blk(r), :], p[...]))
    xk = nt(e[...], p[...])
    wk[0:FIX, 0:NODES] = nt(e[0:FIX, :], k[...])
    factors_in(flag, 1, (f["p"], f["q"]), (f["po"], f["qo"]), p)
    factors_in(flag, 1, (f["k"], f["j"]), (f["ko"], f["jo"]), k)
    put(xh, xl, 2 * NODES, xk + nt(g[...], p[...]))
    wk[0:FIX, NODES : 2 * NODES] = nt(g[0:FIX, :], k[...])
    wk[0:FIX, 2 * NODES : 2 * NODES + 2 * FIX] = nt(e[0:FIX, :], e[...]) + nt(g[0:FIX, :], g[...])
    for r in range(2 * PARTS):
        put(xh, xl, NODES + r * LANES, nt(k[blk(r), :], p[...]))
    first_w(f, 1, k, w2)


def load_next_x(flag, which, f, xh, xl):
    for r in range(PARTS):
        own, got = f["x"][blk(r), :], f["y"][blk(r), :]
        put(xh, xl, which * NODES + r * LANES, jnp.where(flag, *((own, got) if which == 0 else (got, own))))
        own, got = f["xo"][blk(r), :], f["yo"][blk(r), :]
        value = jnp.where(flag, *((own, got) if which == 0 else (got, own)))
        put(xh, xl, which * NODES + HALF + r * LANES, turned(value))


def load_next_w(flag, which, f, w):
    is_own = flag if which == 0 else jnp.logical_not(flag)

    @pl.when(is_own)
    def _():
        w[...] = f["w"][...]

    @pl.when(jnp.logical_not(is_own))
    def _():
        for r in range(PARTS):
            for s in range(2 * PARTS):
                w[blk(r), blk(s)] = unpack_block(
                    lambda i: f["v"][i], lambda i: f["vo"][i], r, s
                )


def load_next_k(flag, f, xh, xl, wk):
    at = slice(HALF, HALF + FIX)
    put(xh, xl, 2 * NODES, jnp.concatenate(
        [f["x"][at, :] + f["y"][at, :], turned(f["xo"][at, :] + f["yo"][at, :])], axis=0
    ))
    at = slice(HALF + FIX, HALF + 2 * FIX)
    own, got = f["x"][at, :], f["y"][at, :]
    wk[0:FIX, 0:NODES] = jnp.where(flag, own, got)
    wk[0:FIX, NODES : 2 * NODES] = jnp.where(flag, got, own)
    at = slice(HALF + 2 * FIX, HALF + 3 * FIX)
    wk[0:FIX, 2 * NODES : 2 * NODES + LANES] = f["x"][at, 0:LANES] + f["y"][at, 0:LANES]


def joined_logs(f, l_ref):
    at = slice(HALF + 2 * FIX, HALF + 3 * FIX)
    logs = jnp.broadcast_to(l_ref[0:1, :], (FIX, LANES))
    if "x" in f:
        logs = logs + (f["x"][at, LANES : 2 * LANES] + f["y"][at, LANES : 2 * LANES])
    return logs


def pivot_kernel(names, flag_ref, hi, lo, *refs):
    f = dict(zip(names, refs))
    out, xh, xl, ch, cl, w1, *more = refs[len(names) :]
    flag = flag_ref[0] == 1
    if "p" in f:
        load_first_1(flag, f, xh, xl, w1, *more)
    else:
        load_next_x(flag, 0, f, xh, xl)
        load_next_w(flag, 0, f, w1)
    solve_rows(xh, xl, 0, HALF, hi, lo, ch, cl)
    for cs, value in products(ch, cl, 0, HALF, xh, xl, 0, NODES):
        w1[:, cs] = w1[:, cs] - value
    pack(out, w1)


def rest_kernel(names, flag_ref, hi, lo, l_ref, *refs):
    f = dict(zip(names, refs))
    cpl, rr, packed, xh, xl, ch, cl, w2, wk, *more = refs[len(names) :]
    flag = flag_ref[0] == 1
    if "p" in f:
        load_first_2(flag, f, xh, xl, w2, wk, *more)
    else:
        load_next_x(flag, 0, f, xh, xl)
        load_next_x(flag, 1, f, xh, xl)
        load_next_w(flag, 1, f, w2)
        load_next_k(flag, f, xh, xl, wk)
    solve_rows(xh, xl, NODES, HALF, hi, lo, ch, cl)
    solve_rows(xh, xl, 2 * NODES, FIX, hi, lo, ch, cl)
    for cs, value in products(ch, cl, NODES, HALF, xh, xl, 0, NODES):
        cpl[0:HALF, cs] = -value
    for cs, value in products(ch, cl, NODES, HALF, xh, xl, NODES, NODES):
        rr[:, cs] = w2[:, cs] - value
    at = 2 * NODES
    for s in range(2):
        rows = slice(HALF + s * FIX, HALF + (s + 1) * FIX)
        cpl[rows, :] = wk[:, s * NODES : (s + 1) * NODES]
        for cs, value in products(ch, cl, at, FIX, xh, xl, s * NODES, NODES):
            cpl[rows, cs] = cpl[rows, cs] - value
    last = slice(HALF + 2 * FIX, HALF + 3 * FIX)
    cpl[last, :] = jnp.zeros((FIX, NODES), F32)
    for cs, value in products(ch, cl, at, FIX, xh, xl, at, 2 * FIX):
        cpl[last, cs] = wk[:, at : at + 2 * FIX] - value
    cpl[last, LANES : 2 * LANES] = joined_logs(f, l_ref)
    pack(packed, rr)


def final_kernel(names, flag_ref, hi, lo, l_ref, *refs):
    f = dict(zip(names, refs))
    ends, arrow, logs, xh, xl, ch, cl, w1, w2, wk, t_ref = refs[len(names) :]
    flag = flag_ref[0] == 1
    core = flag_ref[1]
    load_next_x(flag, 0, f, xh, xl)
    load_next_x(flag, 1, f, xh, xl)
    load_next_w(flag, 0, f, w1)
    load_next_w(flag, 1, f, w2)
    load_next_k(flag, f, xh, xl, wk)
    solve_rows(xh, xl, 0, HALF, hi, lo, ch, cl)
    solve_rows(xh, xl, NODES, HALF, hi, lo, ch, cl)
    solve_rows(xh, xl, 2 * NODES, FIX, hi, lo, ch, cl)
    own = core * HALF
    far = (1 - core) * HALF

    def place(dst, value, base):
        dst[:, pl.ds(pl.multiple_of(own + base, LANES), HALF)] = value[:, :HALF]
        dst[:, pl.ds(pl.multiple_of(far + base, LANES), HALF)] = value[:, HALF:]

    for b in range(2):
        for s in range(2):
            for cs, value in products(ch, cl, b * NODES, HALF, xh, xl, s * NODES, NODES):
                if b == s:
                    w = (w1, w2)[b]
                    w[:, cs] = w[:, cs] - value
                else:
                    t_ref[:, cs] = -value
            place(ends.at[b], (w1, w2)[b][...] if b == s else t_ref[...], s * NODES)
    at = 2 * NODES
    for s in range(2):
        for cs, value in products(ch, cl, at, FIX, xh, xl, s * NODES, NODES):
            t_ref[0:FIX, cs] = wk[:, slice(s * NODES + cs.start, s * NODES + cs.stop)] - value
        place(arrow, t_ref[0:FIX, :], s * NODES)
    ((cs, value),) = products(ch, cl, at, FIX, xh, xl, at, 2 * FIX)
    value = wk[:, at : at + 2 * FIX] - value
    swapped = jnp.concatenate([value[:, FIX:], value[:, :FIX]], axis=1)
    arrow[:, at : at + 2 * FIX] = jnp.where(core == 0, value, swapped)
    logs[...] = joined_logs(f, l_ref)[0:TILE, :]


SMEM = pl.BlockSpec(memory_space=pltpu.SMEM)
VMEM = pl.BlockSpec(memory_space=pltpu.VMEM)


def shape(*dims, dtype=F32):
    return jax.ShapeDtypeStruct(dims, dtype)


def launch(kernel, name, flops, out, scratch, args, scalars=None):
    held = sum(a.size * a.dtype.itemsize for a in (*args, *jax.tree.leaves(out), *scratch))
    specs = [VMEM] * len(args)
    if scalars is not None:
        specs, args = [SMEM] + specs, [scalars] + list(args)
    return pl.pallas_call(
        kernel,
        out_shape=out,
        in_specs=specs,
        out_specs=jax.tree.map(lambda _: VMEM, out),
        scratch_shapes=[pltpu.VMEM(s.shape, s.dtype) for s in scratch],
        compiler_params=pltpu.CompilerParams(vmem_limit_bytes=(60 << 20) if scalars is None else held + (4 << 20)),
        cost_estimate=pl.CostEstimate(
            flops=flops, bytes_accessed=8 << 20, transcendentals=NODES
        ),
        name=name,
    )(*args)


PACKED = shape(12, LANES, LANES)
SQUARE = shape(NODES, NODES)
SQUARE16 = shape(NODES, NODES, dtype=BF16)
ROWS = shape(HALF, NODES)
STACK16 = shape(2 * (NODES + FIX), NODES, dtype=BF16)
WIDE = shape(FIX, 2 * NODES + LANES)
EFF16 = shape(2 * FIX, NODES, dtype=BF16)
INV_SCRATCH = (
    SQUARE,
    shape(NODES, 2 * LANES, dtype=BF16),
    shape(2 * LANES, NODES, dtype=BF16),
    shape(LANES, NODES, dtype=BF16),
    shape(LANES, NODES),
    shape(LANES, LANES),
)
INV_OUT = (SQUARE16, SQUARE16, shape(TILE, LANES))


def shards(spatial, transition, effect, diag):
    steps = lax.axis_size("tm")
    index = lax.axis_index("tm")
    core = lax.axis_index("blk")
    bit = [(index // 2**r) % 2 for r in range(3)]

    def other(x):
        return lax.ppermute(x, "blk", [(0, 1), (1, 0)])

    def partner(x, level):
        if level == 1:
            pairs = [(t, (t // 4) * 4 + 3 - t % 4) for t in range(steps)]
        else:
            pairs = [(t, t ^ (1, 2, 4)[level]) for t in range(steps)]
        return lax.ppermute(x, "tm", pairs)

    def scalars(flag):
        return jnp.stack([flag.astype(jnp.int32), core.astype(jnp.int32)])

    lower = bit[0] == 0
    f = {}
    diag_got = partner(diag, 0)
    f["p"] = jnp.where(lower, transition, spatial)
    f["q"] = partner(f["p"], 0)
    f["po"] = other(f["p"])
    pivot_diag = jnp.where(lower, diag_got, diag)
    pivot_diag = jnp.concatenate([pivot_diag, other(pivot_diag)])[None]
    keep_diag = jnp.where(lower, diag, diag_got)
    after = bit[1] == 1
    f["d"] = jnp.stack([jnp.where(after, keep_diag, 0.0), jnp.where(after, 0.0, keep_diag)])
    keep = jnp.where(lower, spatial, transition)
    f["q"], pivot_diag, keep, effect = lax.optimization_barrier((f["q"], pivot_diag, keep, effect))
    f["qo"] = other(f["q"])
    f["k"] = keep
    f["j"] = partner(keep, 0)
    f["e"] = effect
    f["g"] = partner(effect, 0)
    hi, lo, logs = launch(
        first_inverse_kernel,
        "first_inverse",
        30_000_000_000,
        INV_OUT,
        INV_SCRATCH + (shape(NODES, 2 * NODES, dtype=BF16),),
        [f["p"], f["q"], f["po"], f["qo"], pivot_diag],
    )
    f["ko"], f["eo"] = other(f["k"]), other(f["e"])
    f["j"], f["g"], logs = lax.optimization_barrier((f["j"], f["g"], logs))
    f["jo"], f["go"] = other(f["j"]), other(f["g"])
    flags = scalars(bit[0] != bit[1])
    rest_extra = (SQUARE16, SQUARE16, EFF16, EFF16)
    for level in (1, 2):
        names = [n for n in f]
        args = [f[n] for n in names]
        extra = (SQUARE16, SQUARE16) if level == 1 else ()
        piece = launch(
            functools.partial(pivot_kernel, names),
            "pivot%d" % level,
            5_000_000_000,
            PACKED,
            (STACK16, STACK16, STACK16, STACK16, ROWS) + extra,
            [hi, lo] + args,
            flags,
        )
        piece_got = partner(piece, level)
        piece_other = other(piece)
        cpl, rr, packed = launch(
            functools.partial(rest_kernel, names),
            "rest%d" % level,
            9_000_000_000,
            (shape(HALF + 3 * FIX, NODES), ROWS, PACKED),
            (STACK16, STACK16, STACK16, STACK16, ROWS, WIDE)
            + (rest_extra if level == 1 else ()),
            [hi, lo, logs] + args,
            flags,
        )
        piece_got, cpl = lax.optimization_barrier((piece_got, cpl))
        piece_got_other = other(piece_got)
        f = {"x": cpl, "y": partner(cpl, level), "xo": other(cpl)}
        f["w"] = rr
        f["v"] = partner(packed, level)
        hi, lo, logs = launch(
            next_inverse_kernel,
            "inverse%d" % level,
            30_000_000_000,
            INV_OUT,
            INV_SCRATCH,
            [piece, piece_got, piece_other, piece_got_other],
        )
        f["y"], f["v"], logs = lax.optimization_barrier((f["y"], f["v"], logs))
        f["yo"] = other(f["y"])
        f["vo"] = other(f["v"])
        flags = scalars(bit[2] == 0 if level == 2 else bit[1] != bit[2])
    names = [n for n in f]
    ends, arrow, logs = launch(
        functools.partial(final_kernel, names),
        "final",
        20_000_000_000,
        (shape(2, HALF, 2 * NODES), shape(FIX, 2 * (NODES + FIX)), shape(TILE, LANES)),
        (STACK16, STACK16, STACK16, STACK16, ROWS, ROWS, WIDE, ROWS),
        [hi, lo, logs] + [f[n] for n in names],
        flags,
    )
    return ends[None], arrow[None], (logs[0, 0:1] / (7 * NODES))


def solution(mesh):
    return jax.shard_map(
        shards,
        mesh=mesh,
        in_specs=(
            P(("tm", "blk"), None),
            P(("tm", "blk"), None),
            P(("tm", "blk"), None),
            P(("tm", "blk")),
        ),
        out_specs=(P("tm", None, "blk", None), P("tm", "blk", None), P("tm")),
        check_vma=False,
    )
```

```python
import functools

import jax
import jax.numpy as jnp
from jax import lax
from jax.experimental import pallas as pl
from jax.experimental.pallas import tpu as pltpu
from jax.sharding import PartitionSpec as P

F32 = jnp.float32
BF16 = jnp.bfloat16
TILE = 8
LANES = 128


def split(x):
    high = x.astype(BF16)
    return high, (x - high.astype(F32)).astype(BF16)


def nn(a, b):
    return jnp.dot(a, b, preferred_element_type=F32)


def dot3(a, b):
    return nn(a[0], b[0]) + (nn(a[0], b[1]) + nn(a[1], b[0]))


def rows8(v, q):
    return jnp.broadcast_to(v[q : q + 1, :], (TILE, LANES))


def lane8(v, j):
    return jnp.broadcast_to(v[:, j : j + 1], (TILE, LANES))


SUBS = 2 * TILE


def solve16(own, p, lane, sub):
    at = SUBS * p
    inside = (lane >= at) & (lane < at + SUBS)
    cols = [[lane8(own[t], at + j) for t in range(2)] for j in range(SUBS)]
    cur = [jnp.where(inside, (lane - at - TILE * t == sub).astype(F32), own[t]) for t in range(2)]
    dets = []
    for q in range(0, SUBS, 2):
        tq, sq = q // TILE, q % TILE
        first, second = sub == sq, sub == sq + 1
        either = first | second
        a, b = rows8(cols[q][tq], sq), rows8(cols[q + 1][tq], sq)
        d, c = rows8(cols[q][tq], sq + 1), rows8(cols[q + 1][tq], sq + 1)
        det = a * c - b * d
        dets.append(det[0:1])
        inv = pltpu.reciprocal(det, approx=True)
        f, g = list(cols[q]), list(cols[q + 1])
        f[tq] = jnp.where(first, -1.0, jnp.where(second, 0.0, f[tq]))
        g[tq] = jnp.where(second, -1.0, jnp.where(first, 0.0, g[tq]))

        def apply(v):
            x, y = rows8(v[tq], sq), rows8(v[tq], sq + 1)
            u, w = c * x - b * y, a * y - d * x
            base = [jnp.where(either, 0.0, v[t]) if t == tq else v[t] for t in range(2)]
            return [base[t] - (f[t] * u + g[t] * w) * inv for t in range(2)]

        for j in range(q + 2, SUBS):
            cols[j] = apply(cols[j])
        cur = apply(cur)
    return cur, dets, inside


def invert128(tiles):
    lane = lax.broadcasted_iota(jnp.int32, (TILE, LANES), 1)
    sub = lax.broadcasted_iota(jnp.int32, (TILE, LANES), 0)
    logs = jnp.zeros((1, LANES), F32)
    width = 2 * SUBS
    for g in range(LANES // width):
        panel = list(tiles[4 * g : 4 * g + 4])
        for s in range(2):
            p = 2 * g + s
            cur, dets, inside = solve16(panel[2 * s : 2 * s + 2], p, lane, sub)
            for det in dets:
                logs = logs + jnp.log(det)
            spread = [rows8(cur[m // TILE], m % TILE) for m in range(SUBS)]
            new = list(panel)
            for i in range(4):
                if i // 2 == s:
                    new[i] = cur[i % 2]
                    continue
                parts = [lane8(panel[i], SUBS * p + m) * spread[m] for m in range(SUBS)]
                while len(parts) > 1:
                    parts = [parts[m] + parts[m + 1] for m in range(0, len(parts), 2)]
                new[i] = jnp.where(inside, 0.0, panel[i]) - parts[0]
            panel = new
        high, low = split(jnp.concatenate(panel, 0))
        left = split(jnp.concatenate(tiles, 0))

        def padded(v):
            parts = [v]
            if g:
                parts.insert(0, jnp.zeros((width * g, LANES), BF16))
            if width * (g + 1) < LANES:
                parts.append(jnp.zeros((LANES - width * (g + 1), LANES), BF16))
            return jnp.concatenate(parts, 0)

        right = padded(high)
        update = nn(jnp.concatenate(left, 1), jnp.concatenate([right, right], 0))
        update = update + nn(left[0], padded(low))
        inside = (lane >= width * g) & (lane < width * (g + 1))
        tiles = [
            panel[i - 4 * g]
            if 4 * g <= i < 4 * g + 4
            else jnp.where(inside, 0.0, tiles[i]) - update[TILE * i : TILE * i + TILE]
            for i in range(LANES // TILE)
        ]
    return tiles, logs


HALF = 384
NODES = 2 * HALF
FIX = 32
PARTS = HALF // LANES


def nt(a, b):
    return lax.dot_general(a, b, (((1,), (1,)), ((), ())), preferred_element_type=F32)


def nt3(a, b):
    return nt(a[0], b[0]) + (nt(a[0], b[1]) + nt(a[1], b[0]))


def diag_slot(r, s):
    return r * (r + 1) // 2 + s


def off_slot(r, s):
    return 6 + s * (s + 1) // 2 + r


def blk(r):
    return slice(r * LANES, r * LANES + LANES)


def pack(dst, value):
    for r in range(PARTS):
        for s in range(PARTS):
            if r >= s:
                dst[diag_slot(r, s)] = value[blk(r), blk(s)]
            if r <= s:
                dst[off_slot(r, s)] = value[blk(r), HALF + s * LANES : HALF + (s + 1) * LANES]


def unpack_block(mine, theirs, r, s):
    if s < PARTS:
        return mine(diag_slot(r, s)) if r >= s else mine(diag_slot(s, r)).T
    s -= PARTS
    return mine(off_slot(r, s)) if r <= s else theirs(off_slot(s, r)).T


def eliminate(o_ref, hi_ref, lo_ref, l_ref, col, top, low, u_ref, d_ref):
    size = o_ref.shape[0]
    count = size // LANES
    col[...] = jnp.zeros(col.shape, BF16)
    top[...] = jnp.zeros(top.shape, BF16)
    low[...] = jnp.zeros(low.shape, BF16)
    u_ref[...] = o_ref[0:LANES, :]
    d_ref[...] = o_ref[0:LANES, 0:LANES]

    def late_update():
        for j in range(count):
            update = nn(col[...], top[:, blk(j)]) + nn(col[:, 0:LANES], low[:, blk(j)])
            o_ref[:, blk(j)] = o_ref[:, blk(j)] - update

    def at(k):
        return pl.ds(pl.multiple_of(k * LANES, LANES), LANES)

    def body(k, logs):
        ks, before, after = at(k), at(jnp.maximum(k - 1, 0)), at(jnp.minimum(k + 1, count - 1))
        late_update()
        tiles, more = invert128([d_ref[TILE * i : TILE * i + TILE, :] for i in range(LANES // TILE)])
        o_ref[before, :] = u_ref[...]
        block = jnp.concatenate(tiles, 0)
        parts = split(block)
        wide = jnp.concatenate(parts, 1)

        def solve(right):
            return nn(wide, jnp.concatenate([right[0], right[0]], 0)) + nn(parts[0], right[1])

        high, rest = split(o_ref[:, ks])
        col[:, 0:LANES] = high
        col[:, LANES : 2 * LANES] = rest
        ahead = split(solve(split(o_ref[ks, after])))
        left = col[after, :]
        update = nn(left, jnp.concatenate([ahead[0], ahead[0]], 0)) + nn(left[:, 0:LANES], ahead[1])
        d_ref[...] = o_ref[after, after] - update
        u_ref[...] = solve(split(o_ref[ks, :]))
        u_ref[:, ks] = block
        high, rest = split(u_ref[...])
        top[0:LANES, :] = high
        top[LANES : 2 * LANES, :] = high
        low[...] = rest
        o_ref[:, ks] = jnp.zeros((size, LANES), F32)
        return logs + more

    logs = lax.fori_loop(0, count, body, jnp.zeros((1, LANES), F32))
    late_update()
    o_ref[size - LANES : size, :] = u_ref[...]
    l_ref[...] = jnp.broadcast_to(logs, (TILE, LANES))
    for r in range(count):
        high, rest = split(o_ref[blk(r), :])
        hi_ref[blk(r), :] = high
        lo_ref[blk(r), :] = rest


def first_inverse_kernel(p_ref, q_ref, po_ref, qo_ref, d_ref, hi_ref, lo_ref, l_ref, m_ref, *more):
    *more, s_ref = more
    s_ref[:HALF, :NODES] = p_ref[...]
    s_ref[:HALF, NODES:] = q_ref[...]
    s_ref[HALF:, :NODES] = po_ref[...]
    s_ref[HALF:, NODES:] = qo_ref[...]
    eye = lax.broadcasted_iota(jnp.int32, (LANES, LANES), 0) == lax.broadcasted_iota(
        jnp.int32, (LANES, LANES), 1
    )
    for r in range(2 * PARTS):
        m_ref[blk(r), :] = nt(s_ref[blk(r), :], s_ref[...])
        m_ref[blk(r), blk(r)] += jnp.where(eye, d_ref[0:1, blk(r)], 0.0)
    eliminate(m_ref, hi_ref, lo_ref, l_ref, *more)


def next_inverse_kernel(p_ref, q_ref, po_ref, qo_ref, hi_ref, lo_ref, l_ref, m_ref, *more):
    mine = lambda i: p_ref[i] + q_ref[i]
    theirs = lambda i: po_ref[i] + qo_ref[i]
    for r in range(PARTS):
        for s in range(2 * PARTS):
            block = unpack_block(mine, theirs, r, s)
            m_ref[blk(r), blk(s)] = block
            if s >= PARTS:
                m_ref[blk(s), blk(r)] = block.T
        for s in range(r + 1):
            block = theirs(diag_slot(r, s))
            m_ref[blk(PARTS + r), blk(PARTS + s)] = block
            if s < r:
                m_ref[blk(PARTS + s), blk(PARTS + r)] = block.T
    eliminate(m_ref, hi_ref, lo_ref, l_ref, *more)


class Moves:
    def __init__(self, sems):
        self.sems, self.count, self.open = sems, 0, {}

    def take(self):
        self.count += 1
        return self.sems.at[self.count - 1]

    def copy(self, key, src, dst):
        move = pltpu.make_async_copy(src, dst, self.take())
        move.start()
        self.open[key] = move

    def pick(self, key, flag, a, b, dst):
        sem = self.take()
        first = pltpu.make_async_copy(a, dst, sem)
        second = pltpu.make_async_copy(b, dst, sem)

        @pl.when(flag)
        def _():
            first.start()

        @pl.when(jnp.logical_not(flag))
        def _():
            second.start()

        self.open[key] = first

    def wait(self, *keys):
        for key in keys:
            self.open.pop(key).wait()


def put(xh, xl, at, value):
    rows = value.shape[0]
    high, low = split(value)
    xh[at : at + rows, :] = high
    xl[at : at + rows, :] = low


def turned(x):
    return jnp.concatenate([x[:, HALF:], x[:, :HALF]], axis=1)


CHUNK = 256


def solve_rows(xh, xl, at, rows, hi, lo, ch, cl):
    rs = slice(at, at + rows)
    for n in range(0, NODES, CHUNK):
        cs = slice(n, n + CHUNK)
        high, low = split(dot3((xh[rs, :], xl[rs, :]), (hi[:, cs], lo[:, cs])))
        ch[rs, cs] = high
        cl[rs, cs] = low


def products(ch, cl, at, rows, xh, xl, start, count):
    rs = slice(at, at + rows)
    for n in range(0, count, CHUNK):
        width = min(CHUNK, count - n)
        cs = slice(start + n, start + n + width)
        yield slice(n, n + width), nt3((ch[rs, :], cl[rs, :]), (xh[cs, :], xl[cs, :]))


def first_w(d, which, k, w):
    eye = lax.broadcasted_iota(jnp.int32, (LANES, LANES), 0) == lax.broadcasted_iota(
        jnp.int32, (LANES, LANES), 1
    )
    for n in range(0, NODES, CHUNK):
        w[:, n : n + CHUNK] = nt(k[0:HALF, :], k[n : n + CHUNK, :])
    for r in range(PARTS):
        w[blk(r), blk(r)] += jnp.where(eye, d[which : which + 1, blk(r)], 0.0)


def factor_moves(moves, key, flag, which, f, names, dst):
    n = f[names[0]].shape[0]
    for side in range(2):
        pair = [f[name + "o" * side] for name in names]
        a, b = pair if which == 0 else pair[::-1]
        moves.pick(key + "ab"[side], flag, a, b, dst.at[side * n : side * n + n])


def coupling_moves(moves, key, flag, which, f, dst):
    for side in range(2):
        pair = [f[name + "o" * side].at[0:HALF] for name in "xy"]
        a, b = pair if which == 0 else pair[::-1]
        moves.pick(key + "ab"[side], flag, a, b, dst.at[side * HALF : side * HALF + HALF])


def put_coupling(moves, key, buf, which, xh, xl):
    moves.wait(key + "a")
    for r in range(PARTS):
        put(xh, xl, which * NODES + r * LANES, buf[blk(r), :])
    moves.wait(key + "b")
    for r in range(PARTS):
        value = buf[HALF + r * LANES : HALF + (r + 1) * LANES, :]
        put(xh, xl, which * NODES + HALF + r * LANES, turned(value))


def put_small(buf, xh, xl, wk, flag):
    at = slice(0, FIX)
    put(xh, xl, 2 * NODES, jnp.concatenate(
        [buf[0, at, :] + buf[1, at, :], turned(buf[2, at, :] + buf[3, at, :])], axis=0
    ))
    at = slice(FIX, 2 * FIX)
    own, got = buf[0, at, :], buf[1, at, :]
    wk[0:FIX, 0:NODES] = jnp.where(flag, own, got)
    wk[0:FIX, NODES : 2 * NODES] = jnp.where(flag, got, own)
    at = slice(2 * FIX, 3 * FIX)
    wk[0:FIX, 2 * NODES : 2 * NODES + LANES] = buf[0, at, 0:LANES] + buf[1, at, 0:LANES]


def small_moves(moves, f, buf):
    for i, name in enumerate(("x", "y", "xo", "yo")):
        moves.copy("s%d" % i, f[name].at[HALF : HALF + 3 * FIX], buf.at[i])


def unpack_rows(v, vo, w):
    for r in range(PARTS):
        for s in range(2 * PARTS):
            w[blk(r), blk(s)] = unpack_block(lambda i: v[i], lambda i: vo[i], r, s)


def joined_logs(buf, l_ref):
    logs = jnp.broadcast_to(l_ref[0:1, :], (FIX, LANES))
    if buf is not None:
        at = slice(2 * FIX, 3 * FIX)
        logs = logs + (buf[0, at, LANES : 2 * LANES] + buf[1, at, LANES : 2 * LANES])
    return logs


def pivot_first_kernel(names, flag_ref, hi_any, lo_any, *refs):
    f = dict(zip(names, refs))
    out, sems, hi, lo, xh, xl, ch, cl, w1, p, k, d = refs[len(names) :]
    flag = flag_ref[0] == 1
    moves = Moves(sems)
    factor_moves(moves, "k", flag, 0, f, "kj", k)
    factor_moves(moves, "p", flag, 0, f, "pq", p)
    moves.copy("d", f["d"], d)
    moves.copy("hi", hi_any, hi)
    moves.copy("lo", lo_any, lo)
    moves.wait("ka", "kb", "pa", "pb")
    for r in range(2 * PARTS):
        put(xh, xl, r * LANES, nt(k[blk(r), :], p[...]))
    moves.wait("d")
    first_w(d, 0, k, w1)
    moves.wait("hi", "lo")
    solve_rows(xh, xl, 0, HALF, hi, lo, ch, cl)
    for cs, value in products(ch, cl, 0, HALF, xh, xl, 0, NODES):
        w1[:, cs] = w1[:, cs] - value
    pack(out, w1)


def pivot_next_kernel(names, flag_ref, hi_any, lo_any, *refs):
    f = dict(zip(names, refs))
    out, sems, hi, lo, xh, xl, ch, cl, w1, x = refs[len(names) :]
    flag = flag_ref[0] == 1
    moves = Moves(sems)
    coupling_moves(moves, "x", flag, 0, f, x)
    moves.copy("hi", hi_any, hi)
    moves.copy("lo", lo_any, lo)
    moves.copy("w", f["w"], w1)
    put_coupling(moves, "x", x, 0, xh, xl)
    moves.wait("hi", "lo")
    solve_rows(xh, xl, 0, HALF, hi, lo, ch, cl)
    moves.wait("w")
    for cs, value in products(ch, cl, 0, HALF, xh, xl, 0, NODES):
        w1[:, cs] = jnp.where(flag, w1[:, cs], 0.0) - value
    pack(out, w1)


def rest_tail(hi, lo, xh, xl, ch, cl, w2, wk, cpl, rr, packed, logs):
    solve_rows(xh, xl, NODES, HALF, hi, lo, ch, cl)
    solve_rows(xh, xl, 2 * NODES, FIX, hi, lo, ch, cl)
    for cs, value in products(ch, cl, NODES, HALF, xh, xl, 0, NODES):
        cpl[0:HALF, cs] = -value
    for cs, value in products(ch, cl, NODES, HALF, xh, xl, NODES, NODES):
        rr[:, cs] = w2[:, cs] - value
    at = 2 * NODES
    for s in range(2):
        rows = slice(HALF + s * FIX, HALF + (s + 1) * FIX)
        cpl[rows, :] = wk[:, s * NODES : (s + 1) * NODES]
        for cs, value in products(ch, cl, at, FIX, xh, xl, s * NODES, NODES):
            cpl[rows, cs] = cpl[rows, cs] - value
    last = slice(HALF + 2 * FIX, HALF + 3 * FIX)
    cpl[last, :] = jnp.zeros((FIX, NODES), F32)
    for cs, value in products(ch, cl, at, FIX, xh, xl, at, 2 * FIX):
        cpl[last, cs] = wk[:, at : at + 2 * FIX] - value
    cpl[last, LANES : 2 * LANES] = logs
    pack(packed, rr)


def rest_first_kernel(names, flag_ref, hi_any, lo_any, l_ref, *refs):
    f = dict(zip(names, refs))
    cpl, rr, packed, sems, hi, lo, xh, xl, ch, cl, w2, wk, p, k, p2, k2, e, g, d = refs[len(names) :]
    flag = flag_ref[0] == 1
    moves = Moves(sems)
    factor_moves(moves, "p", flag, 0, f, "pq", p)
    factor_moves(moves, "k", flag, 0, f, "kj", k)
    factor_moves(moves, "e", flag, 0, f, "eg", e)
    factor_moves(moves, "g", flag, 1, f, "eg", g)
    factor_moves(moves, "P", flag, 1, f, "pq", p2)
    factor_moves(moves, "K", flag, 1, f, "kj", k2)
    moves.copy("d", f["d"], d)
    moves.copy("hi", hi_any, hi)
    moves.copy("lo", lo_any, lo)
    moves.wait("pa", "pb", "ka", "kb", "ea", "eb", "ga", "gb")
    for r in range(2 * PARTS):
        put(xh, xl, r * LANES, nt(k[blk(r), :], p[...]))
    wk[0:FIX, 0:NODES] = nt(e[0:FIX, :], k[...])
    wk[0:FIX, 2 * NODES : 2 * NODES + 2 * FIX] = nt(e[0:FIX, :], e[...]) + nt(g[0:FIX, :], g[...])
    moves.wait("Pa", "Pb", "Ka", "Kb")
    put(xh, xl, 2 * NODES, nt(e[...], p[...]) + nt(g[...], p2[...]))
    wk[0:FIX, NODES : 2 * NODES] = nt(g[0:FIX, :], k2[...])
    for r in range(2 * PARTS):
        put(xh, xl, NODES + r * LANES, nt(k2[blk(r), :], p2[...]))
    moves.wait("d")
    first_w(d, 1, k2, w2)
    moves.wait("hi", "lo")
    rest_tail(hi, lo, xh, xl, ch, cl, w2, wk, cpl, rr, packed, joined_logs(None, l_ref))


def rest_next_kernel(names, flag_ref, hi_any, lo_any, l_ref, *refs):
    f = dict(zip(names, refs))
    cpl, rr, packed, sems, hi, lo, xh, xl, ch, cl, w2, wk, x, z, small, v, vo = refs[len(names) :]
    flag = flag_ref[0] == 1
    moves = Moves(sems)
    coupling_moves(moves, "z", flag, 1, f, z)
    small_moves(moves, f, small)
    moves.copy("hi", hi_any, hi)
    moves.copy("lo", lo_any, lo)
    coupling_moves(moves, "x", flag, 0, f, x)
    moves.copy("w", f["w"], w2)
    moves.copy("v", f["v"], v)
    moves.copy("vo", f["vo"], vo)
    put_coupling(moves, "z", z, 1, xh, xl)
    moves.wait("s0", "s1", "s2", "s3")
    put_small(small, xh, xl, wk, flag)
    put_coupling(moves, "x", x, 0, xh, xl)
    moves.wait("hi", "lo", "w", "v", "vo")

    @pl.when(flag)
    def _():
        unpack_rows(v, vo, w2)

    rest_tail(hi, lo, xh, xl, ch, cl, w2, wk, cpl, rr, packed, joined_logs(small, l_ref))


def halves(core, b):
    return [pl.multiple_of(side * HALF + b * NODES, LANES) for side in (core, 1 - core)]


def final_kernel(names, flag_ref, hi_any, lo_any, l_ref, *refs):
    f = dict(zip(names, refs))
    ends, part, arrow, logs, sems, outs, hi, lo, xh, xl, ch, cl, w, wk, x, z, small, *bufs = refs[
        len(names) :
    ]
    flag = flag_ref[0] == 1
    core = flag_ref[1]
    moves = Moves(sems)
    coupling_moves(moves, "x", flag, 0, f, x)
    moves.copy("hi", hi_any, hi)
    moves.copy("lo", lo_any, lo)
    coupling_moves(moves, "z", flag, 1, f, z)
    small_moves(moves, f, small)
    moves.copy("w", f["w"], w)
    put_coupling(moves, "x", x, 0, xh, xl)
    moves.wait("hi", "lo")
    solve_rows(xh, xl, 0, HALF, hi, lo, ch, cl)
    put_coupling(moves, "z", z, 1, xh, xl)
    solve_rows(xh, xl, NODES, HALF, hi, lo, ch, cl)
    moves.wait("w", "s0", "s1", "s2", "s3")
    put_small(small, xh, xl, wk, flag)
    solve_rows(xh, xl, 2 * NODES, FIX, hi, lo, ch, cl)
    waits = []
    for i, (b, s) in enumerate(((0, 0), (1, 1), (0, 1), (1, 0))):
        buf = bufs[i]
        for cs, value in products(ch, cl, b * NODES, HALF, xh, xl, s * NODES, NODES):
            buf[:, cs] = -value
        sources = [buf.at[:, 0:HALF], buf.at[:, HALF:NODES]]
        places = [ends.at[b, :, pl.ds(at, HALF)] for at in halves(core, s)]
        out = [pltpu.make_async_copy(sources[h], places[h], outs.at[2 * i + h]) for h in range(2)]
        waits += out
        if b != s:
            for move in out:
                move.start()
            continue
        native = flag if b == 0 else jnp.logical_not(flag)

        @pl.when(native)
        def _():
            buf[...] = buf[...] + w[...]
            for move in out:
                move.start()

        @pl.when(jnp.logical_not(native))
        def _():
            for h in range(2):
                pltpu.make_async_copy(
                    sources[h], part.at[:, h * HALF : (h + 1) * HALF], outs.at[2 * i + h]
                ).start()

    at = 2 * NODES
    for s in range(2):
        own, far = halves(core, s)
        for cs, value in products(ch, cl, at, FIX, xh, xl, s * NODES, NODES):
            wk[:, slice(s * NODES + cs.start, s * NODES + cs.stop)] -= value
        arrow[:, pl.ds(own, HALF)] = wk[:, s * NODES : s * NODES + HALF]
        arrow[:, pl.ds(far, HALF)] = wk[:, s * NODES + HALF : (s + 1) * NODES]
    ((cs, value),) = products(ch, cl, at, FIX, xh, xl, at, 2 * FIX)
    value = wk[:, at : at + 2 * FIX] - value
    swapped = jnp.concatenate([value[:, FIX:], value[:, :FIX]], axis=1)
    arrow[:, at : at + 2 * FIX] = jnp.where(core == 0, value, swapped)
    logs[...] = joined_logs(small, l_ref)[0:TILE, :]
    for move in waits:
        move.wait()


def finish_kernel(flag_ref, ends_in, part, v, vo, ends, outs, buf):
    core = flag_ref[1]
    block = flag_ref[0]
    unpack_rows(v, vo, buf)
    buf[...] = buf[...] + part[...]
    moves = []
    for h, side in enumerate((core, 1 - core)):
        at = pl.multiple_of(side * HALF + block * NODES, LANES)
        moves.append(
            pltpu.make_async_copy(
                buf.at[:, h * HALF : (h + 1) * HALF],
                ends.at[block, :, pl.ds(at, HALF)],
                outs.at[h],
            )
        )
        moves[-1].start()
    for move in moves:
        move.wait()


SMEM = pl.BlockSpec(memory_space=pltpu.SMEM)
VMEM = pl.BlockSpec(memory_space=pltpu.VMEM)


def shape(*dims, dtype=F32):
    return jax.ShapeDtypeStruct(dims, dtype)


ANY = pl.BlockSpec(memory_space=pl.ANY)


def launch(kernel, name, flops, out, scratch, args, scalars=None, specs=None, out_specs=None, alias=None):
    specs = specs or [VMEM] * len(args)
    if scalars is not None:
        specs, args = [SMEM] + specs, [scalars] + list(args)
    return pl.pallas_call(
        kernel,
        out_shape=out,
        in_specs=specs,
        out_specs=out_specs or jax.tree.map(lambda _: VMEM, out),
        scratch_shapes=[
            pltpu.VMEM(s.shape, s.dtype) if isinstance(s, jax.ShapeDtypeStruct) else s
            for s in scratch
        ],
        compiler_params=pltpu.CompilerParams(vmem_limit_bytes=60 << 20),
        cost_estimate=pl.CostEstimate(
            flops=flops, bytes_accessed=8 << 20, transcendentals=NODES
        ),
        input_output_aliases=alias or {},
        name=name,
    )(*args)


PACKED = shape(12, LANES, LANES)
SQUARE = shape(NODES, NODES)
SQUARE16 = shape(NODES, NODES, dtype=BF16)
ROWS = shape(HALF, NODES)
STACK16 = shape(2 * (NODES + FIX), NODES, dtype=BF16)
WIDE = shape(FIX, 2 * NODES + LANES)
SEMS = pltpu.SemaphoreType.DMA((24,))
X_ROWS = shape(NODES, NODES)
SMALL = shape(4, 3 * FIX, NODES)
DIAG = shape(2, HALF)
BOTH16 = (SQUARE16, SQUARE16)
STACKS = (SEMS,) + BOTH16 + (STACK16,) * 4
EFF16 = shape(2 * FIX, NODES, dtype=BF16)
INV_SCRATCH = (
    SQUARE,
    shape(NODES, 2 * LANES, dtype=BF16),
    shape(2 * LANES, NODES, dtype=BF16),
    shape(LANES, NODES, dtype=BF16),
    shape(LANES, NODES),
    shape(LANES, LANES),
)
INV_OUT = (SQUARE16, SQUARE16, shape(TILE, LANES))


def shards(spatial, transition, effect, diag):
    steps = lax.axis_size("tm")
    index = lax.axis_index("tm")
    core = lax.axis_index("blk")
    bit = [(index // 2**r) % 2 for r in range(3)]

    def other(x):
        return lax.ppermute(x, "blk", [(0, 1), (1, 0)])

    def partner(x, level):
        if level == 1:
            pairs = [(t, (t // 4) * 4 + 3 - t % 4) for t in range(steps)]
        else:
            pairs = [(t, t ^ (1, 2, 4)[level]) for t in range(steps)]
        return lax.ppermute(x, "tm", pairs)

    def scalars(flag):
        return jnp.stack([flag.astype(jnp.int32), core.astype(jnp.int32)])

    lower = bit[0] == 0
    f = {}
    diag_got = partner(diag, 0)
    f["p"] = jnp.where(lower, transition, spatial)
    f["q"] = partner(f["p"], 0)
    f["po"] = other(f["p"])
    pivot_diag = jnp.where(lower, diag_got, diag)
    pivot_diag = jnp.concatenate([pivot_diag, other(pivot_diag)])[None]
    keep_diag = jnp.where(lower, diag, diag_got)
    after = bit[1] == 1
    f["d"] = jnp.stack([jnp.where(after, keep_diag, 0.0), jnp.where(after, 0.0, keep_diag)])
    keep = jnp.where(lower, spatial, transition)
    f["q"], pivot_diag, keep, effect = lax.optimization_barrier((f["q"], pivot_diag, keep, effect))
    f["qo"] = other(f["q"])
    f["k"] = keep
    f["j"] = partner(keep, 0)
    f["e"] = effect
    f["g"] = partner(effect, 0)
    hi, lo, logs = launch(
        first_inverse_kernel,
        "first_inverse",
        30_000_000_000,
        INV_OUT,
        INV_SCRATCH + (shape(NODES, 2 * NODES, dtype=BF16),),
        [f["p"], f["q"], f["po"], f["qo"], pivot_diag],
    )
    f["ko"], f["eo"] = other(f["k"]), other(f["e"])
    f["j"], f["g"], logs = lax.optimization_barrier((f["j"], f["g"], logs))
    f["jo"], f["go"] = other(f["j"]), other(f["g"])
    flags = scalars(bit[0] != bit[1])
    for level in (1, 2):
        names = [n for n in f]
        args = [f[n] for n in names]
        first = level == 1
        piece = launch(
            functools.partial(pivot_first_kernel if first else pivot_next_kernel, names),
            "pivot%d" % level,
            5_000_000_000,
            PACKED,
            STACKS + (ROWS,) + (BOTH16 + (DIAG,) if first else (X_ROWS,)),
            [hi, lo] + args,
            flags,
            [ANY] * (2 + len(args)),
        )
        if not first:
            packed_got, piece = lax.optimization_barrier((packed_got, piece))
            piece = piece + jnp.where(flags[0] == 1, 0.0, packed_got)
            f["v"] = packed_got
            f["vo"] = other(packed_got)
            names, args = names + ["v", "vo"], args + [f["v"], f["vo"]]
        piece_got = partner(piece, level)
        piece_other = other(piece)
        cpl, rr, packed = launch(
            functools.partial(rest_first_kernel if first else rest_next_kernel, names),
            "rest%d" % level,
            9_000_000_000,
            (shape(HALF + 3 * FIX, NODES), ROWS, PACKED),
            STACKS
            + (ROWS, WIDE)
            + (BOTH16 * 2 + (EFF16, EFF16, DIAG) if first else (X_ROWS, X_ROWS, SMALL, PACKED, PACKED)),
            [hi, lo, logs] + args,
            flags,
            [ANY, ANY, VMEM] + [ANY] * len(args),
        )
        piece_got, cpl = lax.optimization_barrier((piece_got, cpl))
        piece_got_other = other(piece_got)
        f = {"x": cpl, "y": partner(cpl, level), "xo": other(cpl), "w": rr}
        hi, lo, logs = launch(
            next_inverse_kernel,
            "inverse%d" % level,
            30_000_000_000,
            INV_OUT,
            INV_SCRATCH,
            [piece, piece_got, piece_other, piece_got_other],
        )
        f["y"], packed, logs = lax.optimization_barrier((f["y"], packed, logs))
        packed_got = partner(packed, level)
        f["yo"] = other(f["y"])
        flags = scalars(bit[2] == 0 if level == 2 else bit[1] != bit[2])
    names = [n for n in f]
    ends, part, arrow, logs = launch(
        functools.partial(final_kernel, names),
        "final",
        20_000_000_000,
        (shape(2, HALF, 2 * NODES), ROWS, shape(FIX, 2 * (NODES + FIX)), shape(TILE, LANES)),
        (SEMS, pltpu.SemaphoreType.DMA((8,))) + STACKS[1:] + (ROWS, WIDE, X_ROWS, X_ROWS, SMALL) + (ROWS,) * 4,
        [hi, lo, logs] + [f[n] for n in names],
        flags,
        [ANY, ANY, VMEM] + [ANY] * len(names),
        (ANY, ANY, VMEM, VMEM),
    )
    packed_got, part = lax.optimization_barrier((packed_got, part))
    ends = launch(
        finish_kernel,
        "finish",
        1_000_000_000,
        shape(2, HALF, 2 * NODES),
        (pltpu.SemaphoreType.DMA((2,)), ROWS),
        [ends, part, packed_got, other(packed_got)],
        flags,
        [ANY, VMEM, VMEM, VMEM],
        ANY,
        {1: 0},
    )
    return ends[None], arrow[None], (logs[0, 0:1] / (7 * NODES))


def solution(mesh):
    return jax.shard_map(
        shards,
        mesh=mesh,
        in_specs=(
            P(("tm", "blk"), None),
            P(("tm", "blk"), None),
            P(("tm", "blk"), None),
            P(("tm", "blk")),
        ),
        out_specs=(P("tm", None, "blk", None), P("tm", "blk", None), P("tm")),
        check_vma=False,
    )
```

```python
import functools

import jax
import jax.numpy as jnp
from jax import lax
from jax.experimental import pallas as pl
from jax.experimental.pallas import tpu as pltpu
from jax.sharding import PartitionSpec as P

F32 = jnp.float32
BF16 = jnp.bfloat16
TILE = 8
LANES = 128


def split(x):
    high = x.astype(BF16)
    return high, (x - high.astype(F32)).astype(BF16)


def nn(a, b):
    return jnp.dot(a, b, preferred_element_type=F32)


def dot3(a, b):
    return nn(a[0], b[0]) + (nn(a[0], b[1]) + nn(a[1], b[0]))


def rows8(v, q):
    return jnp.broadcast_to(v[q : q + 1, :], (TILE, LANES))


def lane8(v, j):
    return jnp.broadcast_to(v[:, j : j + 1], (TILE, LANES))


SUBS = 2 * TILE


def solve16(own, p, lane, sub):
    at = SUBS * p
    inside = (lane >= at) & (lane < at + SUBS)
    cols = [[lane8(own[t], at + j) for t in range(2)] for j in range(SUBS)]
    cur = [jnp.where(inside, (lane - at - TILE * t == sub).astype(F32), own[t]) for t in range(2)]
    dets = []
    for q in range(0, SUBS, 2):
        tq, sq = q // TILE, q % TILE
        first, second = sub == sq, sub == sq + 1
        either = first | second
        a, b = rows8(cols[q][tq], sq), rows8(cols[q + 1][tq], sq)
        d, c = rows8(cols[q][tq], sq + 1), rows8(cols[q + 1][tq], sq + 1)
        det = a * c - b * d
        dets.append(det[0:1])
        inv = pltpu.reciprocal(det, approx=True)
        f, g = list(cols[q]), list(cols[q + 1])
        f[tq] = jnp.where(first, -1.0, jnp.where(second, 0.0, f[tq]))
        g[tq] = jnp.where(second, -1.0, jnp.where(first, 0.0, g[tq]))

        def apply(v):
            x, y = rows8(v[tq], sq), rows8(v[tq], sq + 1)
            u, w = c * x - b * y, a * y - d * x
            base = [jnp.where(either, 0.0, v[t]) if t == tq else v[t] for t in range(2)]
            return [base[t] - (f[t] * u + g[t] * w) * inv for t in range(2)]

        for j in range(q + 2, SUBS):
            cols[j] = apply(cols[j])
        cur = apply(cur)
    return cur, dets, inside


def invert128(tiles):
    lane = lax.broadcasted_iota(jnp.int32, (TILE, LANES), 1)
    sub = lax.broadcasted_iota(jnp.int32, (TILE, LANES), 0)
    logs = jnp.zeros((1, LANES), F32)
    width = 2 * SUBS
    for g in range(LANES // width):
        panel = list(tiles[4 * g : 4 * g + 4])
        for s in range(2):
            p = 2 * g + s
            cur, dets, inside = solve16(panel[2 * s : 2 * s + 2], p, lane, sub)
            for m in range(0, len(dets), 4):
                quad = (dets[m] * dets[m + 1]) * (dets[m + 2] * dets[m + 3])
                logs = logs + jnp.log(quad)
            spread = [rows8(cur[m // TILE], m % TILE) for m in range(SUBS)]
            new = list(panel)
            for i in range(4):
                if i // 2 == s:
                    new[i] = cur[i % 2]
                    continue
                parts = [lane8(panel[i], SUBS * p + m) * spread[m] for m in range(SUBS)]
                while len(parts) > 1:
                    parts = [parts[m] + parts[m + 1] for m in range(0, len(parts), 2)]
                new[i] = jnp.where(inside, 0.0, panel[i]) - parts[0]
            panel = new
        high, low = split(jnp.concatenate(panel, 0))
        left = split(jnp.concatenate(tiles, 0))

        def padded(v):
            parts = [v]
            if g:
                parts.insert(0, jnp.zeros((width * g, LANES), BF16))
            if width * (g + 1) < LANES:
                parts.append(jnp.zeros((LANES - width * (g + 1), LANES), BF16))
            return jnp.concatenate(parts, 0)

        right = padded(high)
        update = nn(jnp.concatenate(left, 1), jnp.concatenate([right, right], 0))
        update = update + nn(left[0], padded(low))
        inside = (lane >= width * g) & (lane < width * (g + 1))
        tiles = [
            panel[i - 4 * g]
            if 4 * g <= i < 4 * g + 4
            else jnp.where(inside, 0.0, tiles[i]) - update[TILE * i : TILE * i + TILE]
            for i in range(LANES // TILE)
        ]
    return tiles, logs


CHUNK = 256
HALF = 384
NODES = 2 * HALF
FIX = 32
PARTS = HALF // LANES


def nt(a, b):
    return lax.dot_general(a, b, (((1,), (1,)), ((), ())), preferred_element_type=F32)


def nt3(a, b):
    return nt(a[0], b[0]) + (nt(a[0], b[1]) + nt(a[1], b[0]))


def diag_slot(r, s):
    return r * (r + 1) // 2 + s


def off_slot(r, s):
    return 6 + s * (s + 1) // 2 + r


def blk(r):
    return slice(r * LANES, r * LANES + LANES)


def pack(dst, value):
    for r in range(PARTS):
        for s in range(PARTS):
            if r >= s:
                dst[diag_slot(r, s)] = value[blk(r), blk(s)]
            if r <= s:
                dst[off_slot(r, s)] = value[blk(r), HALF + s * LANES : HALF + (s + 1) * LANES]


def unpack_block(mine, theirs, r, s):
    if s < PARTS:
        return mine(diag_slot(r, s)) if r >= s else mine(diag_slot(s, r)).T
    s -= PARTS
    return mine(off_slot(r, s)) if r <= s else theirs(off_slot(s, r)).T


def eliminate(o_ref, hi_ref, lo_ref, l_ref, col, top, low, u_ref, d_ref):
    size = o_ref.shape[0]
    count = size // LANES
    col[...] = jnp.zeros(col.shape, BF16)
    top[...] = jnp.zeros(top.shape, BF16)
    low[...] = jnp.zeros(low.shape, BF16)
    u_ref[...] = o_ref[0:LANES, :]
    d_ref[...] = o_ref[0:LANES, 0:LANES]

    def late_update():
        for n in range(0, size, CHUNK):
            cs = slice(n, n + CHUNK)
            update = nn(col[...], top[:, cs]) + nn(col[:, 0:LANES], low[:, cs])
            o_ref[:, cs] = o_ref[:, cs] - update

    def at(k):
        return pl.ds(pl.multiple_of(k * LANES, LANES), LANES)

    def body(k, logs):
        ks, before, after = at(k), at(jnp.maximum(k - 1, 0)), at(jnp.minimum(k + 1, count - 1))
        late_update()
        tiles, more = invert128([d_ref[TILE * i : TILE * i + TILE, :] for i in range(LANES // TILE)])
        o_ref[before, :] = u_ref[...]
        block = jnp.concatenate(tiles, 0)
        parts = split(block)
        wide = jnp.concatenate(parts, 1)

        def solve(right):
            return nn(wide, jnp.concatenate([right[0], right[0]], 0)) + nn(parts[0], right[1])

        high, rest = split(o_ref[:, ks])
        col[:, 0:LANES] = high
        col[:, LANES : 2 * LANES] = rest
        ahead = split(solve(split(o_ref[ks, after])))
        left = col[after, :]
        update = nn(left, jnp.concatenate([ahead[0], ahead[0]], 0)) + nn(left[:, 0:LANES], ahead[1])
        d_ref[...] = o_ref[after, after] - update
        u_ref[...] = solve(split(o_ref[ks, :]))
        u_ref[:, ks] = block
        high, rest = split(u_ref[...])
        top[0:LANES, :] = high
        top[LANES : 2 * LANES, :] = high
        low[...] = rest
        o_ref[:, ks] = jnp.zeros((size, LANES), F32)
        return logs + more

    logs = lax.fori_loop(0, count, body, jnp.zeros((1, LANES), F32))
    late_update()
    o_ref[size - LANES : size, :] = u_ref[...]
    l_ref[...] = jnp.broadcast_to(logs, (TILE, LANES))
    for r in range(count):
        high, rest = split(o_ref[blk(r), :])
        hi_ref[blk(r), :] = high
        lo_ref[blk(r), :] = rest


def first_inverse_kernel(p_ref, q_ref, po_ref, qo_ref, d_ref, hi_ref, lo_ref, l_ref, m_ref, *more):
    *more, s_ref = more
    s_ref[:HALF, :NODES] = p_ref[...]
    s_ref[:HALF, NODES:] = q_ref[...]
    s_ref[HALF:, :NODES] = po_ref[...]
    s_ref[HALF:, NODES:] = qo_ref[...]
    eye = lax.broadcasted_iota(jnp.int32, (LANES, LANES), 0) == lax.broadcasted_iota(
        jnp.int32, (LANES, LANES), 1
    )
    for n in range(0, NODES, CHUNK):
        m_ref[:, n : n + CHUNK] = nt(s_ref[...], s_ref[n : n + CHUNK, :])
    for r in range(2 * PARTS):
        m_ref[blk(r), blk(r)] += jnp.where(eye, d_ref[0:1, blk(r)], 0.0)
    eliminate(m_ref, hi_ref, lo_ref, l_ref, *more)


def next_inverse_kernel(p_ref, q_ref, po_ref, qo_ref, hi_ref, lo_ref, l_ref, m_ref, *more):
    mine = lambda i: p_ref[i] + q_ref[i]
    theirs = lambda i: po_ref[i] + qo_ref[i]
    for r in range(PARTS):
        for s in range(2 * PARTS):
            block = unpack_block(mine, theirs, r, s)
            m_ref[blk(r), blk(s)] = block
            if s >= PARTS:
                m_ref[blk(s), blk(r)] = block.T
        for s in range(r + 1):
            block = theirs(diag_slot(r, s))
            m_ref[blk(PARTS + r), blk(PARTS + s)] = block
            if s < r:
                m_ref[blk(PARTS + s), blk(PARTS + r)] = block.T
    eliminate(m_ref, hi_ref, lo_ref, l_ref, *more)


class Moves:
    def __init__(self, sems):
        self.sems, self.count, self.open = sems, 0, {}

    def take(self):
        self.count += 1
        return self.sems.at[self.count - 1]

    def copy(self, key, src, dst):
        move = pltpu.make_async_copy(src, dst, self.take())
        move.start()
        self.open[key] = move

    def pick(self, key, flag, a, b, dst):
        sem = self.take()
        first = pltpu.make_async_copy(a, dst, sem)
        second = pltpu.make_async_copy(b, dst, sem)

        @pl.when(flag)
        def _():
            first.start()

        @pl.when(jnp.logical_not(flag))
        def _():
            second.start()

        self.open[key] = first

    def wait(self, *keys):
        for key in keys:
            self.open.pop(key).wait()


def put(xh, xl, at, value):
    rows = value.shape[0]
    high, low = split(value)
    xh[at : at + rows, :] = high
    xl[at : at + rows, :] = low


def put_product(xh, xl, at, a, b):
    rows = slice(at, at + a.shape[0])
    for n in range(0, NODES, CHUNK):
        high, low = split(nt(a[...], b[n : n + CHUNK, :]))
        xh[rows, n : n + CHUNK] = high
        xl[rows, n : n + CHUNK] = low


def turned(x):
    return jnp.concatenate([x[:, HALF:], x[:, :HALF]], axis=1)


def solve_rows(xh, xl, at, rows, hi, lo, ch, cl):
    rs = slice(at, at + rows)
    for n in range(0, NODES, CHUNK):
        cs = slice(n, n + CHUNK)
        high, low = split(dot3((xh[rs, :], xl[rs, :]), (hi[:, cs], lo[:, cs])))
        ch[rs, cs] = high
        cl[rs, cs] = low


def products(ch, cl, at, rows, xh, xl, start, count):
    rs = slice(at, at + rows)
    for n in range(0, count, CHUNK):
        width = min(CHUNK, count - n)
        cs = slice(start + n, start + n + width)
        yield slice(n, n + width), nt3((ch[rs, :], cl[rs, :]), (xh[cs, :], xl[cs, :]))


def first_w(d, which, k, w):
    eye = lax.broadcasted_iota(jnp.int32, (LANES, LANES), 0) == lax.broadcasted_iota(
        jnp.int32, (LANES, LANES), 1
    )
    for n in range(0, NODES, CHUNK):
        w[:, n : n + CHUNK] = nt(k[0:HALF, :], k[n : n + CHUNK, :])
    for r in range(PARTS):
        w[blk(r), blk(r)] += jnp.where(eye, d[which : which + 1, blk(r)], 0.0)


def factor_moves(moves, key, flag, which, f, names, dst):
    n = f[names[0]].shape[0]
    for side in range(2):
        pair = [f[name + "o" * side] for name in names]
        a, b = pair if which == 0 else pair[::-1]
        moves.pick(key + "ab"[side], flag, a, b, dst.at[side * n : side * n + n])


def coupling_moves(moves, key, flag, which, f, dst):
    for side in range(2):
        pair = [f[name + "o" * side].at[0:HALF] for name in "xy"]
        a, b = pair if which == 0 else pair[::-1]
        moves.pick(key + "ab"[side], flag, a, b, dst.at[side * HALF : side * HALF + HALF])


def put_coupling(moves, key, buf, which, xh, xl):
    moves.wait(key + "a")
    for r in range(PARTS):
        put(xh, xl, which * NODES + r * LANES, buf[blk(r), :])
    moves.wait(key + "b")
    for r in range(PARTS):
        value = buf[HALF + r * LANES : HALF + (r + 1) * LANES, :]
        put(xh, xl, which * NODES + HALF + r * LANES, turned(value))


def put_small(buf, xh, xl, wk, flag):
    at = slice(0, FIX)
    put(xh, xl, 2 * NODES, jnp.concatenate(
        [buf[0, at, :] + buf[1, at, :], turned(buf[2, at, :] + buf[3, at, :])], axis=0
    ))
    at = slice(FIX, 2 * FIX)
    own, got = buf[0, at, :], buf[1, at, :]
    wk[0:FIX, 0:NODES] = jnp.where(flag, own, got)
    wk[0:FIX, NODES : 2 * NODES] = jnp.where(flag, got, own)
    at = slice(2 * FIX, 3 * FIX)
    wk[0:FIX, 2 * NODES : 2 * NODES + LANES] = buf[0, at, 0:LANES] + buf[1, at, 0:LANES]


def small_moves(moves, f, buf):
    for i, name in enumerate(("x", "y", "xo", "yo")):
        moves.copy("s%d" % i, f[name].at[HALF : HALF + 3 * FIX], buf.at[i])


def unpack_rows(v, vo, w):
    for r in range(PARTS):
        for s in range(2 * PARTS):
            w[blk(r), blk(s)] = unpack_block(lambda i: v[i], lambda i: vo[i], r, s)


def joined_logs(buf, l_ref):
    logs = jnp.broadcast_to(l_ref[0:1, :], (FIX, LANES))
    if buf is not None:
        at = slice(2 * FIX, 3 * FIX)
        logs = logs + (buf[0, at, LANES : 2 * LANES] + buf[1, at, LANES : 2 * LANES])
    return logs


def pivot_first_kernel(names, flag_ref, hi_any, lo_any, *refs):
    f = dict(zip(names, refs))
    out, sems, hi, lo, xh, xl, ch, cl, w1, p, k, d = refs[len(names) :]
    flag = flag_ref[0] == 1
    moves = Moves(sems)
    factor_moves(moves, "k", flag, 0, f, "kj", k)
    factor_moves(moves, "p", flag, 0, f, "pq", p)
    moves.copy("d", f["d"], d)
    moves.copy("hi", hi_any, hi)
    moves.copy("lo", lo_any, lo)
    moves.wait("ka", "kb", "pa", "pb")
    put_product(xh, xl, 0, k, p)
    moves.wait("d")
    first_w(d, 0, k, w1)
    moves.wait("hi", "lo")
    solve_rows(xh, xl, 0, HALF, hi, lo, ch, cl)
    for cs, value in products(ch, cl, 0, HALF, xh, xl, 0, NODES):
        w1[:, cs] = w1[:, cs] - value
    pack(out, w1)


def pivot_next_kernel(names, flag_ref, hi_any, lo_any, *refs):
    f = dict(zip(names, refs))
    out, sems, hi, lo, xh, xl, ch, cl, w1, x = refs[len(names) :]
    flag = flag_ref[0] == 1
    moves = Moves(sems)
    coupling_moves(moves, "x", flag, 0, f, x)
    moves.copy("hi", hi_any, hi)
    moves.copy("lo", lo_any, lo)
    moves.copy("w", f["w"], w1)
    put_coupling(moves, "x", x, 0, xh, xl)
    moves.wait("hi", "lo")
    solve_rows(xh, xl, 0, HALF, hi, lo, ch, cl)
    moves.wait("w")
    for cs, value in products(ch, cl, 0, HALF, xh, xl, 0, NODES):
        w1[:, cs] = jnp.where(flag, w1[:, cs], 0.0) - value
    pack(out, w1)


def rest_tail(hi, lo, xh, xl, ch, cl, w2, wk, cpl, rr, packed, logs):
    solve_rows(xh, xl, NODES, HALF, hi, lo, ch, cl)
    solve_rows(xh, xl, 2 * NODES, FIX, hi, lo, ch, cl)
    for cs, value in products(ch, cl, NODES, HALF, xh, xl, 0, NODES):
        cpl[0:HALF, cs] = -value
    for cs, value in products(ch, cl, NODES, HALF, xh, xl, NODES, NODES):
        rr[:, cs] = w2[:, cs] - value
    at = 2 * NODES
    for s in range(2):
        rows = slice(HALF + s * FIX, HALF + (s + 1) * FIX)
        cpl[rows, :] = wk[:, s * NODES : (s + 1) * NODES]
        for cs, value in products(ch, cl, at, FIX, xh, xl, s * NODES, NODES):
            cpl[rows, cs] = cpl[rows, cs] - value
    last = slice(HALF + 2 * FIX, HALF + 3 * FIX)
    cpl[last, :] = jnp.zeros((FIX, NODES), F32)
    for cs, value in products(ch, cl, at, FIX, xh, xl, at, 2 * FIX):
        cpl[last, cs] = wk[:, at : at + 2 * FIX] - value
    cpl[last, LANES : 2 * LANES] = logs
    pack(packed, rr)


def rest_first_kernel(names, flag_ref, hi_any, lo_any, l_ref, *refs):
    f = dict(zip(names, refs))
    cpl, rr, packed, sems, hi, lo, xh, xl, ch, cl, w2, wk, p, k, p2, k2, e, g, d = refs[len(names) :]
    flag = flag_ref[0] == 1
    moves = Moves(sems)
    factor_moves(moves, "p", flag, 0, f, "pq", p)
    factor_moves(moves, "k", flag, 0, f, "kj", k)
    factor_moves(moves, "e", flag, 0, f, "eg", e)
    factor_moves(moves, "g", flag, 1, f, "eg", g)
    factor_moves(moves, "P", flag, 1, f, "pq", p2)
    factor_moves(moves, "K", flag, 1, f, "kj", k2)
    moves.copy("d", f["d"], d)
    moves.copy("hi", hi_any, hi)
    moves.copy("lo", lo_any, lo)
    moves.wait("pa", "pb", "ka", "kb", "ea", "eb", "ga", "gb")
    put_product(xh, xl, 0, k, p)
    wk[0:FIX, 0:NODES] = nt(e[0:FIX, :], k[...])
    wk[0:FIX, 2 * NODES : 2 * NODES + 2 * FIX] = nt(e[0:FIX, :], e[...]) + nt(g[0:FIX, :], g[...])
    moves.wait("Pa", "Pb", "Ka", "Kb")
    put(xh, xl, 2 * NODES, nt(e[...], p[...]) + nt(g[...], p2[...]))
    wk[0:FIX, NODES : 2 * NODES] = nt(g[0:FIX, :], k2[...])
    put_product(xh, xl, NODES, k2, p2)
    moves.wait("d")
    first_w(d, 1, k2, w2)
    moves.wait("hi", "lo")
    rest_tail(hi, lo, xh, xl, ch, cl, w2, wk, cpl, rr, packed, joined_logs(None, l_ref))


def rest_next_kernel(names, flag_ref, hi_any, lo_any, l_ref, *refs):
    f = dict(zip(names, refs))
    cpl, rr, packed, sems, hi, lo, xh, xl, ch, cl, w2, wk, x, z, small, v, vo = refs[len(names) :]
    flag = flag_ref[0] == 1
    moves = Moves(sems)
    coupling_moves(moves, "z", flag, 1, f, z)
    small_moves(moves, f, small)
    moves.copy("hi", hi_any, hi)
    moves.copy("lo", lo_any, lo)
    coupling_moves(moves, "x", flag, 0, f, x)
    moves.copy("w", f["w"], w2)
    moves.copy("v", f["v"], v)
    moves.copy("vo", f["vo"], vo)
    put_coupling(moves, "z", z, 1, xh, xl)
    moves.wait("s0", "s1", "s2", "s3")
    put_small(small, xh, xl, wk, flag)
    put_coupling(moves, "x", x, 0, xh, xl)
    moves.wait("hi", "lo", "w", "v", "vo")

    @pl.when(flag)
    def _():
        unpack_rows(v, vo, w2)

    rest_tail(hi, lo, xh, xl, ch, cl, w2, wk, cpl, rr, packed, joined_logs(small, l_ref))


def halves(core, b):
    return [pl.multiple_of(side * HALF + b * NODES, LANES) for side in (core, 1 - core)]


def final_kernel(names, flag_ref, hi_any, lo_any, l_ref, *refs):
    f = dict(zip(names, refs))
    ends, part, arrow, logs, sems, outs, hi, lo, xh, xl, ch, cl, w, wk, x, z, small, *bufs = refs[
        len(names) :
    ]
    flag = flag_ref[0] == 1
    core = flag_ref[1]
    moves = Moves(sems)
    coupling_moves(moves, "x", flag, 0, f, x)
    moves.copy("hi", hi_any, hi)
    moves.copy("lo", lo_any, lo)
    coupling_moves(moves, "z", flag, 1, f, z)
    small_moves(moves, f, small)
    moves.copy("w", f["w"], w)
    put_coupling(moves, "x", x, 0, xh, xl)
    moves.wait("hi", "lo")
    solve_rows(xh, xl, 0, HALF, hi, lo, ch, cl)
    put_coupling(moves, "z", z, 1, xh, xl)
    solve_rows(xh, xl, NODES, HALF, hi, lo, ch, cl)
    moves.wait("w", "s0", "s1", "s2", "s3")
    put_small(small, xh, xl, wk, flag)
    solve_rows(xh, xl, 2 * NODES, FIX, hi, lo, ch, cl)
    waits = []
    for i, (b, s) in enumerate(((0, 0), (1, 1), (0, 1), (1, 0))):
        buf = bufs[i]
        for cs, value in products(ch, cl, b * NODES, HALF, xh, xl, s * NODES, NODES):
            buf[:, cs] = -value
        sources = [buf.at[:, 0:HALF], buf.at[:, HALF:NODES]]
        places = [ends.at[b, :, pl.ds(at, HALF)] for at in halves(core, s)]
        out = [pltpu.make_async_copy(sources[h], places[h], outs.at[2 * i + h]) for h in range(2)]
        waits += out
        if b != s:
            for move in out:
                move.start()
            continue
        native = flag if b == 0 else jnp.logical_not(flag)

        @pl.when(native)
        def _():
            buf[...] = buf[...] + w[...]
            for move in out:
                move.start()

        @pl.when(jnp.logical_not(native))
        def _():
            for h in range(2):
                pltpu.make_async_copy(
                    sources[h], part.at[:, h * HALF : (h + 1) * HALF], outs.at[2 * i + h]
                ).start()

    at = 2 * NODES
    for s in range(2):
        own, far = halves(core, s)
        for cs, value in products(ch, cl, at, FIX, xh, xl, s * NODES, NODES):
            wk[:, slice(s * NODES + cs.start, s * NODES + cs.stop)] -= value
        arrow[:, pl.ds(own, HALF)] = wk[:, s * NODES : s * NODES + HALF]
        arrow[:, pl.ds(far, HALF)] = wk[:, s * NODES + HALF : (s + 1) * NODES]
    ((cs, value),) = products(ch, cl, at, FIX, xh, xl, at, 2 * FIX)
    value = wk[:, at : at + 2 * FIX] - value
    swapped = jnp.concatenate([value[:, FIX:], value[:, :FIX]], axis=1)
    arrow[:, at : at + 2 * FIX] = jnp.where(core == 0, value, swapped)
    logs[...] = joined_logs(small, l_ref)[0:TILE, :]
    for move in waits:
        move.wait()


def finish_kernel(flag_ref, ends_in, part, v, vo, ends, outs, buf):
    core = flag_ref[1]
    block = flag_ref[0]
    unpack_rows(v, vo, buf)
    buf[...] = buf[...] + part[...]
    moves = []
    for h, side in enumerate((core, 1 - core)):
        at = pl.multiple_of(side * HALF + block * NODES, LANES)
        moves.append(
            pltpu.make_async_copy(
                buf.at[:, h * HALF : (h + 1) * HALF],
                ends.at[block, :, pl.ds(at, HALF)],
                outs.at[h],
            )
        )
        moves[-1].start()
    for move in moves:
        move.wait()


SMEM = pl.BlockSpec(memory_space=pltpu.SMEM)
VMEM = pl.BlockSpec(memory_space=pltpu.VMEM)


def shape(*dims, dtype=F32):
    return jax.ShapeDtypeStruct(dims, dtype)


ANY = pl.BlockSpec(memory_space=pl.ANY)


def launch(kernel, name, flops, out, scratch, args, scalars=None, specs=None, out_specs=None, alias=None):
    specs = specs or [VMEM] * len(args)
    if scalars is not None:
        specs, args = [SMEM] + specs, [scalars] + list(args)
    return pl.pallas_call(
        kernel,
        out_shape=out,
        in_specs=specs,
        out_specs=out_specs or jax.tree.map(lambda _: VMEM, out),
        scratch_shapes=[
            pltpu.VMEM(s.shape, s.dtype) if isinstance(s, jax.ShapeDtypeStruct) else s
            for s in scratch
        ],
        compiler_params=pltpu.CompilerParams(vmem_limit_bytes=60 << 20),
        cost_estimate=pl.CostEstimate(
            flops=flops, bytes_accessed=8 << 20, transcendentals=NODES
        ),
        input_output_aliases=alias or {},
        name=name,
    )(*args)


PACKED = shape(12, LANES, LANES)
SQUARE = shape(NODES, NODES)
SQUARE16 = shape(NODES, NODES, dtype=BF16)
ROWS = shape(HALF, NODES)
STACK16 = shape(2 * (NODES + FIX), NODES, dtype=BF16)
WIDE = shape(FIX, 2 * NODES + LANES)
SEMS = pltpu.SemaphoreType.DMA((24,))
X_ROWS = shape(NODES, NODES)
SMALL = shape(4, 3 * FIX, NODES)
DIAG = shape(2, HALF)
BOTH16 = (SQUARE16, SQUARE16)
STACKS = (SEMS,) + BOTH16 + (STACK16,) * 4
EFF16 = shape(2 * FIX, NODES, dtype=BF16)
INV_SCRATCH = (
    SQUARE,
    shape(NODES, 2 * LANES, dtype=BF16),
    shape(2 * LANES, NODES, dtype=BF16),
    shape(LANES, NODES, dtype=BF16),
    shape(LANES, NODES),
    shape(LANES, LANES),
)
INV_OUT = (SQUARE16, SQUARE16, shape(TILE, LANES))


def shards(spatial, transition, effect, diag):
    steps = lax.axis_size("tm")
    index = lax.axis_index("tm")
    core = lax.axis_index("blk")
    bit = [(index // 2**r) % 2 for r in range(3)]

    def other(x):
        return lax.ppermute(x, "blk", [(0, 1), (1, 0)])

    def partner(x, level):
        if level == 1:
            pairs = [(t, (t // 4) * 4 + 3 - t % 4) for t in range(steps)]
        else:
            pairs = [(t, t ^ (1, 2, 4)[level]) for t in range(steps)]
        return lax.ppermute(x, "tm", pairs)

    def scalars(flag):
        return jnp.stack([flag.astype(jnp.int32), core.astype(jnp.int32)])

    lower = bit[0] == 0
    f = {}
    diag_got = partner(diag, 0)
    f["p"] = jnp.where(lower, transition, spatial)
    f["q"] = partner(f["p"], 0)
    f["po"] = other(f["p"])
    pivot_diag = jnp.where(lower, diag_got, diag)
    pivot_diag = jnp.concatenate([pivot_diag, other(pivot_diag)])[None]
    keep_diag = jnp.where(lower, diag, diag_got)
    after = bit[1] == 1
    f["d"] = jnp.stack([jnp.where(after, keep_diag, 0.0), jnp.where(after, 0.0, keep_diag)])
    keep = jnp.where(lower, spatial, transition)
    f["q"], pivot_diag, keep, effect = lax.optimization_barrier((f["q"], pivot_diag, keep, effect))
    f["qo"] = other(f["q"])
    f["k"] = keep
    f["j"] = partner(keep, 0)
    f["e"] = effect
    f["g"] = partner(effect, 0)
    hi, lo, logs = launch(
        first_inverse_kernel,
        "first_inverse",
        30_000_000_000,
        INV_OUT,
        INV_SCRATCH + (shape(NODES, 2 * NODES, dtype=BF16),),
        [f["p"], f["q"], f["po"], f["qo"], pivot_diag],
    )
    f["ko"], f["eo"] = other(f["k"]), other(f["e"])
    f["j"], f["g"], logs = lax.optimization_barrier((f["j"], f["g"], logs))
    f["jo"], f["go"] = other(f["j"]), other(f["g"])
    flags = scalars(bit[0] != bit[1])
    for level in (1, 2):
        names = [n for n in f]
        args = [f[n] for n in names]
        first = level == 1
        piece = launch(
            functools.partial(pivot_first_kernel if first else pivot_next_kernel, names),
            "pivot%d" % level,
            5_000_000_000,
            PACKED,
            STACKS + (ROWS,) + (BOTH16 + (DIAG,) if first else (X_ROWS,)),
            [hi, lo] + args,
            flags,
            [ANY] * (2 + len(args)),
        )
        if not first:
            packed_got, piece = lax.optimization_barrier((packed_got, piece))
            piece = piece + jnp.where(flags[0] == 1, 0.0, packed_got)
            f["v"] = packed_got
            f["vo"] = other(packed_got)
            names, args = names + ["v", "vo"], args + [f["v"], f["vo"]]
        piece_got = partner(piece, level)
        piece_other = other(piece)
        cpl, rr, packed = launch(
            functools.partial(rest_first_kernel if first else rest_next_kernel, names),
            "rest%d" % level,
            9_000_000_000,
            (shape(HALF + 3 * FIX, NODES), ROWS, PACKED),
            STACKS
            + (ROWS, WIDE)
            + (BOTH16 * 2 + (EFF16, EFF16, DIAG) if first else (X_ROWS, X_ROWS, SMALL, PACKED, PACKED)),
            [hi, lo, logs] + args,
            flags,
            [ANY, ANY, VMEM] + [ANY] * len(args),
        )
        piece_got, cpl = lax.optimization_barrier((piece_got, cpl))
        piece_got_other = other(piece_got)
        f = {"x": cpl, "y": partner(cpl, level), "xo": other(cpl), "w": rr}
        hi, lo, logs = launch(
            next_inverse_kernel,
            "inverse%d" % level,
            30_000_000_000,
            INV_OUT,
            INV_SCRATCH,
            [piece, piece_got, piece_other, piece_got_other],
        )
        f["y"], packed, logs = lax.optimization_barrier((f["y"], packed, logs))
        packed_got = partner(packed, level)
        f["yo"] = other(f["y"])
        flags = scalars(bit[2] == 0 if level == 2 else bit[1] != bit[2])
    names = [n for n in f]
    ends, part, arrow, logs = launch(
        functools.partial(final_kernel, names),
        "final",
        20_000_000_000,
        (shape(2, HALF, 2 * NODES), ROWS, shape(FIX, 2 * (NODES + FIX)), shape(TILE, LANES)),
        (SEMS, pltpu.SemaphoreType.DMA((8,))) + STACKS[1:] + (ROWS, WIDE, X_ROWS, X_ROWS, SMALL) + (ROWS,) * 4,
        [hi, lo, logs] + [f[n] for n in names],
        flags,
        [ANY, ANY, VMEM] + [ANY] * len(names),
        (ANY, ANY, VMEM, VMEM),
    )
    packed_got, part = lax.optimization_barrier((packed_got, part))
    ends = launch(
        finish_kernel,
        "finish",
        1_000_000_000,
        shape(2, HALF, 2 * NODES),
        (pltpu.SemaphoreType.DMA((2,)), ROWS),
        [ends, part, packed_got, other(packed_got)],
        flags,
        [ANY, VMEM, VMEM, VMEM],
        ANY,
        {1: 0},
    )
    return ends[None], arrow[None], (logs[0, 0:1] / (7 * NODES))


def solution(mesh):
    return jax.shard_map(
        shards,
        mesh=mesh,
        in_specs=(
            P(("tm", "blk"), None),
            P(("tm", "blk"), None),
            P(("tm", "blk"), None),
            P(("tm", "blk")),
        ),
        out_specs=(P("tm", None, "blk", None), P("tm", "blk", None), P("tm")),
        check_vma=False,
    )
```

```python
import functools

import jax
import jax.numpy as jnp
from jax import lax
from jax.experimental import pallas as pl
from jax.experimental.pallas import tpu as pltpu
from jax.sharding import PartitionSpec as P

F32 = jnp.float32
BF16 = jnp.bfloat16
TILE = 8
LANES = 128


def split(x):
    high = x.astype(BF16)
    return high, (x - high.astype(F32)).astype(BF16)


def nn(a, b):
    return jnp.dot(a, b, preferred_element_type=F32)


def dot3(a, b):
    return nn(a[0], b[0]) + (nn(a[0], b[1]) + nn(a[1], b[0]))


def rows8(v, q):
    return jnp.broadcast_to(v[q : q + 1, :], (TILE, LANES))


def lane8(v, j):
    return jnp.broadcast_to(v[:, j : j + 1], (TILE, LANES))


SUBS = 2 * TILE


def solve16(own, p, lane, sub):
    at = SUBS * p
    inside = (lane >= at) & (lane < at + SUBS)
    cols = [[lane8(own[t], at + j) for t in range(2)] for j in range(SUBS)]
    cur = [jnp.where(inside, (lane - at - TILE * t == sub).astype(F32), own[t]) for t in range(2)]
    dets = []
    for q in range(0, SUBS, 2):
        tq, sq = q // TILE, q % TILE
        first, second = sub == sq, sub == sq + 1
        either = first | second
        a, b = rows8(cols[q][tq], sq), rows8(cols[q + 1][tq], sq)
        d, c = rows8(cols[q][tq], sq + 1), rows8(cols[q + 1][tq], sq + 1)
        det = a * c - b * d
        dets.append(det[0:1])
        inv = pltpu.reciprocal(det, approx=True)
        f, g = list(cols[q]), list(cols[q + 1])
        f[tq] = jnp.where(first, -1.0, jnp.where(second, 0.0, f[tq]))
        g[tq] = jnp.where(second, -1.0, jnp.where(first, 0.0, g[tq]))

        def apply(v):
            x, y = rows8(v[tq], sq), rows8(v[tq], sq + 1)
            u, w = c * x - b * y, a * y - d * x
            base = [jnp.where(either, 0.0, v[t]) if t == tq else v[t] for t in range(2)]
            return [base[t] - (f[t] * u + g[t] * w) * inv for t in range(2)]

        for j in range(q + 2, SUBS):
            cols[j] = apply(cols[j])
        cur = apply(cur)
    return cur, dets, inside


def invert128(tiles):
    lane = lax.broadcasted_iota(jnp.int32, (TILE, LANES), 1)
    sub = lax.broadcasted_iota(jnp.int32, (TILE, LANES), 0)
    logs = jnp.zeros((1, LANES), F32)
    width = 2 * SUBS
    for g in range(LANES // width):
        panel = list(tiles[4 * g : 4 * g + 4])
        for s in range(2):
            p = 2 * g + s
            cur, dets, inside = solve16(panel[2 * s : 2 * s + 2], p, lane, sub)
            for m in range(0, len(dets), 4):
                quad = (dets[m] * dets[m + 1]) * (dets[m + 2] * dets[m + 3])
                logs = logs + jnp.log(quad)
            spread = [rows8(cur[m // TILE], m % TILE) for m in range(SUBS)]
            new = list(panel)
            for i in range(4):
                if i // 2 == s:
                    new[i] = cur[i % 2]
                    continue
                parts = [lane8(panel[i], SUBS * p + m) * spread[m] for m in range(SUBS)]
                while len(parts) > 1:
                    parts = [parts[m] + parts[m + 1] for m in range(0, len(parts), 2)]
                new[i] = jnp.where(inside, 0.0, panel[i]) - parts[0]
            panel = new
        high, low = split(jnp.concatenate(panel, 0))
        left = split(jnp.concatenate(tiles, 0))

        def padded(v):
            parts = [v]
            if g:
                parts.insert(0, jnp.zeros((width * g, LANES), BF16))
            if width * (g + 1) < LANES:
                parts.append(jnp.zeros((LANES - width * (g + 1), LANES), BF16))
            return jnp.concatenate(parts, 0)

        right = padded(high)
        update = nn(jnp.concatenate(left, 1), jnp.concatenate([right, right], 0))
        update = update + nn(left[0], padded(low))
        inside = (lane >= width * g) & (lane < width * (g + 1))
        tiles = [
            panel[i - 4 * g]
            if 4 * g <= i < 4 * g + 4
            else jnp.where(inside, 0.0, tiles[i]) - update[TILE * i : TILE * i + TILE]
            for i in range(LANES // TILE)
        ]
    return tiles, logs


CHUNK = 256
HALF = 384
NODES = 2 * HALF
FIX = 32
PARTS = HALF // LANES


def nt(a, b):
    return lax.dot_general(a, b, (((1,), (1,)), ((), ())), preferred_element_type=F32)


def nt3(a, b):
    return nt(a[0], b[0]) + (nt(a[0], b[1]) + nt(a[1], b[0]))


def diag_slot(r, s):
    return r * (r + 1) // 2 + s


def off_slot(r, s):
    return 6 + s * (s + 1) // 2 + r


def blk(r):
    return slice(r * LANES, r * LANES + LANES)


def pack(dst, value):
    for r in range(PARTS):
        for s in range(PARTS):
            if r >= s:
                dst[diag_slot(r, s)] = value[blk(r), blk(s)]
            if r <= s:
                dst[off_slot(r, s)] = value[blk(r), HALF + s * LANES : HALF + (s + 1) * LANES]


def unpack_block(mine, theirs, r, s):
    if s < PARTS:
        return mine(diag_slot(r, s)) if r >= s else mine(diag_slot(s, r)).T
    s -= PARTS
    return mine(off_slot(r, s)) if r <= s else theirs(off_slot(s, r)).T


def eliminate(o_ref, hi_ref, lo_ref, l_ref, col, top, low, u_ref, d_ref):
    size = o_ref.shape[0]
    count = size // LANES
    col[...] = jnp.zeros(col.shape, BF16)
    top[...] = jnp.zeros(top.shape, BF16)
    low[...] = jnp.zeros(low.shape, BF16)
    u_ref[...] = o_ref[0:LANES, :]
    d_ref[...] = o_ref[0:LANES, 0:LANES]

    def late_update():
        for n in range(0, size, CHUNK):
            cs = slice(n, n + CHUNK)
            update = nn(col[...], top[:, cs]) + nn(col[:, 0:LANES], low[:, cs])
            o_ref[:, cs] = o_ref[:, cs] - update

    def at(k):
        return pl.ds(pl.multiple_of(k * LANES, LANES), LANES)

    def body(k, logs):
        ks, before, after = at(k), at(jnp.maximum(k - 1, 0)), at(jnp.minimum(k + 1, count - 1))
        late_update()
        tiles, more = invert128([d_ref[TILE * i : TILE * i + TILE, :] for i in range(LANES // TILE)])
        o_ref[before, :] = u_ref[...]
        block = jnp.concatenate(tiles, 0)
        parts = split(block)
        wide = jnp.concatenate(parts, 1)

        def solve(right):
            return nn(wide, jnp.concatenate([right[0], right[0]], 0)) + nn(parts[0], right[1])

        high, rest = split(o_ref[:, ks])
        col[:, 0:LANES] = high
        col[:, LANES : 2 * LANES] = rest
        ahead = split(solve(split(o_ref[ks, after])))
        left = col[after, :]
        update = nn(left, jnp.concatenate([ahead[0], ahead[0]], 0)) + nn(left[:, 0:LANES], ahead[1])
        d_ref[...] = o_ref[after, after] - update
        u_ref[...] = solve(split(o_ref[ks, :]))
        u_ref[:, ks] = block
        high, rest = split(u_ref[...])
        top[0:LANES, :] = high
        top[LANES : 2 * LANES, :] = high
        low[...] = rest
        o_ref[:, ks] = jnp.zeros((size, LANES), F32)
        return logs + more

    logs = lax.fori_loop(0, count, body, jnp.zeros((1, LANES), F32))
    late_update()
    o_ref[size - LANES : size, :] = u_ref[...]
    l_ref[...] = jnp.broadcast_to(logs, (TILE, LANES))
    for r in range(count):
        high, rest = split(o_ref[blk(r), :])
        hi_ref[blk(r), :] = high
        lo_ref[blk(r), :] = rest


def first_inverse_kernel(p_ref, q_ref, po_ref, qo_ref, d_ref, hi_ref, lo_ref, l_ref, m_ref, *more):
    *more, s_ref = more
    s_ref[:HALF, :NODES] = p_ref[...]
    s_ref[:HALF, NODES:] = q_ref[...]
    s_ref[HALF:, :NODES] = po_ref[...]
    s_ref[HALF:, NODES:] = qo_ref[...]
    eye = lax.broadcasted_iota(jnp.int32, (LANES, LANES), 0) == lax.broadcasted_iota(
        jnp.int32, (LANES, LANES), 1
    )
    for n in range(0, NODES, CHUNK):
        m_ref[:, n : n + CHUNK] = nt(s_ref[...], s_ref[n : n + CHUNK, :])
    for r in range(2 * PARTS):
        m_ref[blk(r), blk(r)] += jnp.where(eye, d_ref[0:1, blk(r)], 0.0)
    eliminate(m_ref, hi_ref, lo_ref, l_ref, *more)


def next_inverse_kernel(p_ref, q_ref, po_ref, qo_ref, hi_ref, lo_ref, l_ref, m_ref, *more):
    mine = lambda i: p_ref[i] + q_ref[i]
    theirs = lambda i: po_ref[i] + qo_ref[i]
    for r in range(PARTS):
        for s in range(2 * PARTS):
            block = unpack_block(mine, theirs, r, s)
            m_ref[blk(r), blk(s)] = block
            if s >= PARTS:
                m_ref[blk(s), blk(r)] = block.T
        for s in range(r + 1):
            block = theirs(diag_slot(r, s))
            m_ref[blk(PARTS + r), blk(PARTS + s)] = block
            if s < r:
                m_ref[blk(PARTS + s), blk(PARTS + r)] = block.T
    eliminate(m_ref, hi_ref, lo_ref, l_ref, *more)


class Moves:
    def __init__(self, sems):
        self.sems, self.count, self.open = sems, 0, {}

    def take(self):
        self.count += 1
        return self.sems.at[self.count - 1]

    def copy(self, key, src, dst):
        move = pltpu.make_async_copy(src, dst, self.take())
        move.start()
        self.open[key] = move

    def pick(self, key, flag, a, b, dst):
        sem = self.take()
        first = pltpu.make_async_copy(a, dst, sem)
        second = pltpu.make_async_copy(b, dst, sem)

        @pl.when(flag)
        def _():
            first.start()

        @pl.when(jnp.logical_not(flag))
        def _():
            second.start()

        self.open[key] = first

    def wait(self, *keys):
        for key in keys:
            self.open.pop(key).wait()


def put(xh, xl, at, value):
    rows = value.shape[0]
    high, low = split(value)
    xh[at : at + rows, :] = high
    xl[at : at + rows, :] = low


def put_product(xh, xl, at, a, b):
    rows = slice(at, at + a.shape[0])
    for n in range(0, NODES, CHUNK):
        high, low = split(nt(a[...], b[n : n + CHUNK, :]))
        xh[rows, n : n + CHUNK] = high
        xl[rows, n : n + CHUNK] = low


def turned(x):
    return jnp.concatenate([x[:, HALF:], x[:, :HALF]], axis=1)


def solve_rows(xh, xl, at, rows, hi, lo, ch, cl):
    rs = slice(at, at + rows)
    for n in range(0, NODES, CHUNK):
        cs = slice(n, n + CHUNK)
        high, low = split(dot3((xh[rs, :], xl[rs, :]), (hi[:, cs], lo[:, cs])))
        ch[rs, cs] = high
        cl[rs, cs] = low


def products(ch, cl, at, rows, xh, xl, start, count):
    rs = slice(at, at + rows)
    for n in range(0, count, CHUNK):
        width = min(CHUNK, count - n)
        cs = slice(start + n, start + n + width)
        yield slice(n, n + width), nt3((ch[rs, :], cl[rs, :]), (xh[cs, :], xl[cs, :]))


def first_w(d, which, k, w):
    eye = lax.broadcasted_iota(jnp.int32, (LANES, LANES), 0) == lax.broadcasted_iota(
        jnp.int32, (LANES, LANES), 1
    )
    for n in range(0, NODES, CHUNK):
        w[:, n : n + CHUNK] = nt(k[0:HALF, :], k[n : n + CHUNK, :])
    for r in range(PARTS):
        w[blk(r), blk(r)] += jnp.where(eye, d[which : which + 1, blk(r)], 0.0)


def factor_moves(moves, key, flag, which, f, names, dst):
    n = f[names[0]].shape[0]
    for side in range(2):
        pair = [f[name + "o" * side] for name in names]
        a, b = pair if which == 0 else pair[::-1]
        moves.pick(key + "ab"[side], flag, a, b, dst.at[side * n : side * n + n])


def coupling_moves(moves, key, flag, which, f, dst):
    for side in range(2):
        pair = [f[name + "o" * side].at[0:HALF] for name in "xy"]
        a, b = pair if which == 0 else pair[::-1]
        moves.pick(key + "ab"[side], flag, a, b, dst.at[side * HALF : side * HALF + HALF])


def put_coupling(moves, key, buf, which, xh, xl):
    moves.wait(key + "a")
    for r in range(PARTS):
        put(xh, xl, which * NODES + r * LANES, buf[blk(r), :])
    moves.wait(key + "b")
    for r in range(PARTS):
        value = buf[HALF + r * LANES : HALF + (r + 1) * LANES, :]
        put(xh, xl, which * NODES + HALF + r * LANES, turned(value))


def put_small(buf, xh, xl, wk, flag):
    at = slice(0, FIX)
    put(xh, xl, 2 * NODES, jnp.concatenate(
        [buf[0, at, :] + buf[1, at, :], turned(buf[2, at, :] + buf[3, at, :])], axis=0
    ))
    at = slice(FIX, 2 * FIX)
    own, got = buf[0, at, :], buf[1, at, :]
    wk[0:FIX, 0:NODES] = jnp.where(flag, own, got)
    wk[0:FIX, NODES : 2 * NODES] = jnp.where(flag, got, own)
    at = slice(2 * FIX, 3 * FIX)
    wk[0:FIX, 2 * NODES : 2 * NODES + LANES] = buf[0, at, 0:LANES] + buf[1, at, 0:LANES]


def small_moves(moves, f, buf):
    for i, name in enumerate(("x", "y", "xo", "yo")):
        moves.copy("s%d" % i, f[name].at[HALF : HALF + 3 * FIX], buf.at[i])


def unpack_rows(v, vo, w):
    for r in range(PARTS):
        for s in range(2 * PARTS):
            w[blk(r), blk(s)] = unpack_block(lambda i: v[i], lambda i: vo[i], r, s)


def joined_logs(buf, l_ref):
    logs = jnp.broadcast_to(l_ref[0:1, :], (FIX, LANES))
    if buf is not None:
        at = slice(2 * FIX, 3 * FIX)
        logs = logs + (buf[0, at, LANES : 2 * LANES] + buf[1, at, LANES : 2 * LANES])
    return logs


def pivot_first_kernel(names, flag_ref, hi_any, lo_any, *refs):
    f = dict(zip(names, refs))
    out, sems, hi, lo, xh, xl, ch, cl, w1, p, k, d = refs[len(names) :]
    flag = flag_ref[0] == 1
    moves = Moves(sems)
    factor_moves(moves, "k", flag, 0, f, "kj", k)
    factor_moves(moves, "p", flag, 0, f, "pq", p)
    moves.copy("d", f["d"], d)
    moves.copy("hi", hi_any, hi)
    moves.copy("lo", lo_any, lo)
    moves.wait("ka", "kb", "pa", "pb")
    put_product(xh, xl, 0, k, p)
    moves.wait("d")
    first_w(d, 0, k, w1)
    moves.wait("hi", "lo")
    solve_rows(xh, xl, 0, HALF, hi, lo, ch, cl)
    for cs, value in products(ch, cl, 0, HALF, xh, xl, 0, NODES):
        w1[:, cs] = w1[:, cs] - value
    pack(out, w1)


def pivot_next_kernel(names, flag_ref, hi_any, lo_any, *refs):
    f = dict(zip(names, refs))
    out, sems, hi, lo, xh, xl, ch, cl, w1, x = refs[len(names) :]
    flag = flag_ref[0] == 1
    moves = Moves(sems)
    coupling_moves(moves, "x", flag, 0, f, x)
    moves.copy("hi", hi_any, hi)
    moves.copy("lo", lo_any, lo)
    moves.copy("w", f["w"], w1)
    put_coupling(moves, "x", x, 0, xh, xl)
    moves.wait("hi", "lo")
    solve_rows(xh, xl, 0, HALF, hi, lo, ch, cl)
    moves.wait("w")
    for cs, value in products(ch, cl, 0, HALF, xh, xl, 0, NODES):
        w1[:, cs] = jnp.where(flag, w1[:, cs], 0.0) - value
    pack(out, w1)


def rest_tail(hi, lo, xh, xl, ch, cl, w2, wk, cpl, rr, packed, logs):
    solve_rows(xh, xl, NODES, HALF, hi, lo, ch, cl)
    solve_rows(xh, xl, 2 * NODES, FIX, hi, lo, ch, cl)
    for cs, value in products(ch, cl, NODES, HALF, xh, xl, 0, NODES):
        cpl[0:HALF, cs] = -value
    for cs, value in products(ch, cl, NODES, HALF, xh, xl, NODES, NODES):
        rr[:, cs] = w2[:, cs] - value
    at = 2 * NODES
    for s in range(2):
        rows = slice(HALF + s * FIX, HALF + (s + 1) * FIX)
        cpl[rows, :] = wk[:, s * NODES : (s + 1) * NODES]
        for cs, value in products(ch, cl, at, FIX, xh, xl, s * NODES, NODES):
            cpl[rows, cs] = cpl[rows, cs] - value
    last = slice(HALF + 2 * FIX, HALF + 3 * FIX)
    cpl[last, :] = jnp.zeros((FIX, NODES), F32)
    for cs, value in products(ch, cl, at, FIX, xh, xl, at, 2 * FIX):
        cpl[last, cs] = wk[:, at : at + 2 * FIX] - value
    cpl[last, LANES : 2 * LANES] = logs
    pack(packed, rr)


def rest_first_kernel(names, flag_ref, hi_any, lo_any, l_ref, *refs):
    f = dict(zip(names, refs))
    cpl, rr, packed, sems, hi, lo, xh, xl, ch, cl, w2, wk, p, k, p2, k2, e, g, d = refs[len(names) :]
    flag = flag_ref[0] == 1
    moves = Moves(sems)
    factor_moves(moves, "p", flag, 0, f, "pq", p)
    factor_moves(moves, "k", flag, 0, f, "kj", k)
    factor_moves(moves, "e", flag, 0, f, "eg", e)
    factor_moves(moves, "g", flag, 1, f, "eg", g)
    factor_moves(moves, "P", flag, 1, f, "pq", p2)
    factor_moves(moves, "K", flag, 1, f, "kj", k2)
    moves.copy("d", f["d"], d)
    moves.copy("hi", hi_any, hi)
    moves.copy("lo", lo_any, lo)
    moves.wait("pa", "pb", "ka", "kb", "ea", "eb", "ga", "gb")
    put_product(xh, xl, 0, k, p)
    wk[0:FIX, 0:NODES] = nt(e[0:FIX, :], k[...])
    wk[0:FIX, 2 * NODES : 2 * NODES + 2 * FIX] = nt(e[0:FIX, :], e[...]) + nt(g[0:FIX, :], g[...])
    moves.wait("Pa", "Pb", "Ka", "Kb")
    put(xh, xl, 2 * NODES, nt(e[...], p[...]) + nt(g[...], p2[...]))
    wk[0:FIX, NODES : 2 * NODES] = nt(g[0:FIX, :], k2[...])
    put_product(xh, xl, NODES, k2, p2)
    moves.wait("d")
    first_w(d, 1, k2, w2)
    moves.wait("hi", "lo")
    rest_tail(hi, lo, xh, xl, ch, cl, w2, wk, cpl, rr, packed, joined_logs(None, l_ref))


def rest_next_kernel(names, flag_ref, hi_any, lo_any, l_ref, *refs):
    f = dict(zip(names, refs))
    cpl, rr, packed, sems, hi, lo, xh, xl, ch, cl, w2, wk, x, z, small, v, vo = refs[len(names) :]
    flag = flag_ref[0] == 1
    moves = Moves(sems)
    coupling_moves(moves, "z", flag, 1, f, z)
    small_moves(moves, f, small)
    moves.copy("hi", hi_any, hi)
    moves.copy("lo", lo_any, lo)
    coupling_moves(moves, "x", flag, 0, f, x)
    moves.copy("w", f["w"], w2)
    moves.copy("v", f["v"], v)
    moves.copy("vo", f["vo"], vo)
    put_coupling(moves, "z", z, 1, xh, xl)
    moves.wait("s0", "s1", "s2", "s3")
    put_small(small, xh, xl, wk, flag)
    put_coupling(moves, "x", x, 0, xh, xl)
    moves.wait("hi", "lo", "w", "v", "vo")

    @pl.when(flag)
    def _():
        unpack_rows(v, vo, w2)

    rest_tail(hi, lo, xh, xl, ch, cl, w2, wk, cpl, rr, packed, joined_logs(small, l_ref))


def halves(core, b):
    return [pl.multiple_of(side * HALF + b * NODES, LANES) for side in (core, 1 - core)]


def final_kernel(names, flag_ref, hi_any, lo_any, l_ref, *refs):
    f = dict(zip(names, refs))
    ends, part, arrow, logs, sems, outs, hi, lo, xh, xl, ch, cl, w, wk, x, z, small, *bufs = refs[
        len(names) :
    ]
    flag = flag_ref[0] == 1
    core = flag_ref[1]
    moves = Moves(sems)
    coupling_moves(moves, "x", flag, 0, f, x)
    moves.copy("hi", hi_any, hi)
    moves.copy("lo", lo_any, lo)
    coupling_moves(moves, "z", flag, 1, f, z)
    small_moves(moves, f, small)
    moves.copy("w", f["w"], w)
    put_coupling(moves, "x", x, 0, xh, xl)
    moves.wait("hi", "lo")
    solve_rows(xh, xl, 0, HALF, hi, lo, ch, cl)
    put_coupling(moves, "z", z, 1, xh, xl)
    solve_rows(xh, xl, NODES, HALF, hi, lo, ch, cl)
    moves.wait("w", "s0", "s1", "s2", "s3")
    put_small(small, xh, xl, wk, flag)
    solve_rows(xh, xl, 2 * NODES, FIX, hi, lo, ch, cl)
    waits = []
    for i, (b, s) in enumerate(((0, 0), (1, 1), (0, 1), (1, 0))):
        buf = bufs[i]
        for cs, value in products(ch, cl, b * NODES, HALF, xh, xl, s * NODES, NODES):
            buf[:, cs] = -value
        sources = [buf.at[:, 0:HALF], buf.at[:, HALF:NODES]]
        places = [ends.at[b, :, pl.ds(at, HALF)] for at in halves(core, s)]
        out = [pltpu.make_async_copy(sources[h], places[h], outs.at[2 * i + h]) for h in range(2)]
        waits += out
        if b != s:
            for move in out:
                move.start()
            continue
        native = flag if b == 0 else jnp.logical_not(flag)

        @pl.when(native)
        def _():
            buf[...] = buf[...] + w[...]
            for move in out:
                move.start()

        @pl.when(jnp.logical_not(native))
        def _():
            for h in range(2):
                pltpu.make_async_copy(
                    sources[h], part.at[:, h * HALF : (h + 1) * HALF], outs.at[2 * i + h]
                ).start()

    at = 2 * NODES
    for s in range(2):
        own, far = halves(core, s)
        for cs, value in products(ch, cl, at, FIX, xh, xl, s * NODES, NODES):
            wk[:, slice(s * NODES + cs.start, s * NODES + cs.stop)] -= value
        arrow[:, pl.ds(own, HALF)] = wk[:, s * NODES : s * NODES + HALF]
        arrow[:, pl.ds(far, HALF)] = wk[:, s * NODES + HALF : (s + 1) * NODES]
    ((cs, value),) = products(ch, cl, at, FIX, xh, xl, at, 2 * FIX)
    value = wk[:, at : at + 2 * FIX] - value
    swapped = jnp.concatenate([value[:, FIX:], value[:, :FIX]], axis=1)
    arrow[:, at : at + 2 * FIX] = jnp.where(core == 0, value, swapped)
    logs[0] = jnp.sum(joined_logs(small, l_ref)[0:1, 0:1]) * (1.0 / (7 * NODES))
    for move in waits:
        move.wait()


def finish_kernel(flag_ref, ends_in, part, v, vo, ends, outs, buf):
    core = flag_ref[1]
    block = flag_ref[0]
    unpack_rows(v, vo, buf)
    buf[...] = buf[...] + part[...]
    moves = []
    for h, side in enumerate((core, 1 - core)):
        at = pl.multiple_of(side * HALF + block * NODES, LANES)
        moves.append(
            pltpu.make_async_copy(
                buf.at[:, h * HALF : (h + 1) * HALF],
                ends.at[block, :, pl.ds(at, HALF)],
                outs.at[h],
            )
        )
        moves[-1].start()
    for move in moves:
        move.wait()


SMEM = pl.BlockSpec(memory_space=pltpu.SMEM)
VMEM = pl.BlockSpec(memory_space=pltpu.VMEM)


def shape(*dims, dtype=F32):
    return jax.ShapeDtypeStruct(dims, dtype)


ANY = pl.BlockSpec(memory_space=pl.ANY)


def launch(kernel, name, flops, out, scratch, args, scalars=None, specs=None, out_specs=None, alias=None):
    specs = specs or [VMEM] * len(args)
    if scalars is not None:
        specs, args = [SMEM] + specs, [scalars] + list(args)
    return pl.pallas_call(
        kernel,
        out_shape=out,
        in_specs=specs,
        out_specs=out_specs or jax.tree.map(lambda _: VMEM, out),
        scratch_shapes=[
            pltpu.VMEM(s.shape, s.dtype) if isinstance(s, jax.ShapeDtypeStruct) else s
            for s in scratch
        ],
        compiler_params=pltpu.CompilerParams(vmem_limit_bytes=60 << 20),
        cost_estimate=pl.CostEstimate(
            flops=flops, bytes_accessed=8 << 20, transcendentals=NODES
        ),
        input_output_aliases=alias or {},
        name=name,
    )(*args)


PACKED = shape(12, LANES, LANES)
SQUARE = shape(NODES, NODES)
SQUARE16 = shape(NODES, NODES, dtype=BF16)
ROWS = shape(HALF, NODES)
STACK16 = shape(2 * (NODES + FIX), NODES, dtype=BF16)
WIDE = shape(FIX, 2 * NODES + LANES)
SEMS = pltpu.SemaphoreType.DMA((24,))
X_ROWS = shape(NODES, NODES)
SMALL = shape(4, 3 * FIX, NODES)
DIAG = shape(2, HALF)
BOTH16 = (SQUARE16, SQUARE16)
STACKS = (SEMS,) + BOTH16 + (STACK16,) * 4
EFF16 = shape(2 * FIX, NODES, dtype=BF16)
INV_SCRATCH = (
    SQUARE,
    shape(NODES, 2 * LANES, dtype=BF16),
    shape(2 * LANES, NODES, dtype=BF16),
    shape(LANES, NODES, dtype=BF16),
    shape(LANES, NODES),
    shape(LANES, LANES),
)
INV_OUT = (SQUARE16, SQUARE16, shape(TILE, LANES))


def shards(spatial, transition, effect, diag):
    steps = lax.axis_size("tm")
    index = lax.axis_index("tm")
    core = lax.axis_index("blk")
    bit = [(index // 2**r) % 2 for r in range(3)]

    def other(x):
        return lax.ppermute(x, "blk", [(0, 1), (1, 0)])

    def partner(x, level):
        if level == 1:
            pairs = [(t, (t // 4) * 4 + 3 - t % 4) for t in range(steps)]
        else:
            pairs = [(t, t ^ (1, 2, 4)[level]) for t in range(steps)]
        return lax.ppermute(x, "tm", pairs)

    def scalars(flag):
        return jnp.stack([flag.astype(jnp.int32), core.astype(jnp.int32)])

    lower = bit[0] == 0
    f = {}
    diag_got = partner(diag, 0)
    f["p"] = jnp.where(lower, transition, spatial)
    f["q"] = partner(f["p"], 0)
    f["po"] = other(f["p"])
    pivot_diag = jnp.where(lower, diag_got, diag)
    pivot_diag = jnp.concatenate([pivot_diag, other(pivot_diag)])[None]
    keep_diag = jnp.where(lower, diag, diag_got)
    after = bit[1] == 1
    f["d"] = jnp.stack([jnp.where(after, keep_diag, 0.0), jnp.where(after, 0.0, keep_diag)])
    keep = jnp.where(lower, spatial, transition)
    all_flags = [
        scalars(flag) for flag in (bit[0] != bit[1], bit[1] != bit[2], bit[2] == 0)
    ]
    f["q"], f["d"], pivot_diag, keep, effect, all_flags = lax.optimization_barrier(
        (f["q"], f["d"], pivot_diag, keep, effect, all_flags)
    )
    f["qo"] = other(f["q"])
    f["k"] = keep
    f["j"] = partner(keep, 0)
    f["e"] = effect
    f["g"] = partner(effect, 0)
    hi, lo, logs = launch(
        first_inverse_kernel,
        "first_inverse",
        30_000_000_000,
        INV_OUT,
        INV_SCRATCH + (shape(NODES, 2 * NODES, dtype=BF16),),
        [f["p"], f["q"], f["po"], f["qo"], pivot_diag],
    )
    f["ko"], f["eo"] = other(f["k"]), other(f["e"])
    f["j"], f["g"], logs = lax.optimization_barrier((f["j"], f["g"], logs))
    f["jo"], f["go"] = other(f["j"]), other(f["g"])
    flags = all_flags[0]
    for level in (1, 2):
        names = [n for n in f]
        args = [f[n] for n in names]
        first = level == 1
        piece = launch(
            functools.partial(pivot_first_kernel if first else pivot_next_kernel, names),
            "pivot%d" % level,
            5_000_000_000,
            PACKED,
            STACKS + (ROWS,) + (BOTH16 + (DIAG,) if first else (X_ROWS,)),
            [hi, lo] + args,
            flags,
            [ANY] * (2 + len(args)),
        )
        if not first:
            packed_got, piece = lax.optimization_barrier((packed_got, piece))
            piece = piece + jnp.where(flags[0] == 1, 0.0, packed_got)
            f["v"] = packed_got
            f["vo"] = other(packed_got)
            names, args = names + ["v", "vo"], args + [f["v"], f["vo"]]
        piece_got = partner(piece, level)
        piece_other = other(piece)
        cpl, rr, packed = launch(
            functools.partial(rest_first_kernel if first else rest_next_kernel, names),
            "rest%d" % level,
            9_000_000_000,
            (shape(HALF + 3 * FIX, NODES), ROWS, PACKED),
            STACKS
            + (ROWS, WIDE)
            + (BOTH16 * 2 + (EFF16, EFF16, DIAG) if first else (X_ROWS, X_ROWS, SMALL, PACKED, PACKED)),
            [hi, lo, logs] + args,
            flags,
            [ANY, ANY, VMEM] + [ANY] * len(args),
        )
        piece_got, cpl = lax.optimization_barrier((piece_got, cpl))
        piece_got_other = other(piece_got)
        f = {"x": cpl, "y": partner(cpl, level), "xo": other(cpl), "w": rr}
        hi, lo, logs = launch(
            next_inverse_kernel,
            "inverse%d" % level,
            30_000_000_000,
            INV_OUT,
            INV_SCRATCH,
            [piece, piece_got, piece_other, piece_got_other],
        )
        f["y"], packed, logs = lax.optimization_barrier((f["y"], packed, logs))
        packed_got = partner(packed, level)
        f["yo"] = other(f["y"])
        flags = all_flags[level]
    names = [n for n in f]
    ends, part, arrow, logs = launch(
        functools.partial(final_kernel, names),
        "final",
        20_000_000_000,
        (shape(2, HALF, 2 * NODES), ROWS, shape(FIX, 2 * (NODES + FIX)), shape(1)),
        (SEMS, pltpu.SemaphoreType.DMA((8,))) + STACKS[1:] + (ROWS, WIDE, X_ROWS, X_ROWS, SMALL) + (ROWS,) * 4,
        [hi, lo, logs] + [f[n] for n in names],
        flags,
        [ANY, ANY, VMEM] + [ANY] * len(names),
        (ANY, ANY, VMEM, SMEM),
    )
    packed_got, part = lax.optimization_barrier((packed_got, part))
    ends = launch(
        finish_kernel,
        "finish",
        1_000_000_000,
        shape(2, HALF, 2 * NODES),
        (pltpu.SemaphoreType.DMA((2,)), ROWS),
        [ends, part, packed_got, other(packed_got)],
        flags,
        [ANY, VMEM, VMEM, VMEM],
        ANY,
        {1: 0},
    )
    return ends[None], arrow[None], logs


def solution(mesh):
    return jax.shard_map(
        shards,
        mesh=mesh,
        in_specs=(
            P(("tm", "blk"), None),
            P(("tm", "blk"), None),
            P(("tm", "blk"), None),
            P(("tm", "blk")),
        ),
        out_specs=(P("tm", None, "blk", None), P("tm", "blk", None), P("tm")),
        check_vma=False,
    )
```

```python
import functools

import jax
import jax.numpy as jnp
from jax import lax
from jax.experimental import pallas as pl
from jax.experimental.pallas import tpu as pltpu
from jax.sharding import PartitionSpec as P

F32 = jnp.float32
BF16 = jnp.bfloat16
TILE = 8
LANES = 128


def split(x):
    high = x.astype(BF16)
    return high, (x - high.astype(F32)).astype(BF16)


def nn(a, b):
    return jnp.dot(a, b, preferred_element_type=F32)


def dot3(a, b):
    return nn(a[0], b[0]) + (nn(a[0], b[1]) + nn(a[1], b[0]))


def rows8(v, q):
    return jnp.broadcast_to(v[q : q + 1, :], (TILE, LANES))


def lane8(v, j):
    return jnp.broadcast_to(v[:, j : j + 1], (TILE, LANES))


SUBS = 2 * TILE


def solve16(own, p, lane, sub):
    at = SUBS * p
    inside = (lane >= at) & (lane < at + SUBS)
    cols = [[lane8(own[t], at + j) for t in range(2)] for j in range(SUBS)]
    cur = [jnp.where(inside, (lane - at - TILE * t == sub).astype(F32), own[t]) for t in range(2)]
    dets = []
    for q in range(0, SUBS, 2):
        tq, sq = q // TILE, q % TILE
        first, second = sub == sq, sub == sq + 1
        either = first | second
        a, b = rows8(cols[q][tq], sq), rows8(cols[q + 1][tq], sq)
        d, c = rows8(cols[q][tq], sq + 1), rows8(cols[q + 1][tq], sq + 1)
        det = a * c - b * d
        dets.append(det[0:1])
        inv = pltpu.reciprocal(det, approx=True)
        f, g = list(cols[q]), list(cols[q + 1])
        f[tq] = jnp.where(first, -1.0, jnp.where(second, 0.0, f[tq]))
        g[tq] = jnp.where(second, -1.0, jnp.where(first, 0.0, g[tq]))

        def apply(v):
            x, y = rows8(v[tq], sq), rows8(v[tq], sq + 1)
            u, w = c * x - b * y, a * y - d * x
            base = [jnp.where(either, 0.0, v[t]) if t == tq else v[t] for t in range(2)]
            return [base[t] - (f[t] * u + g[t] * w) * inv for t in range(2)]

        for j in range(q + 2, SUBS):
            cols[j] = apply(cols[j])
        cur = apply(cur)
    return cur, dets, inside


def invert128(tiles):
    lane = lax.broadcasted_iota(jnp.int32, (TILE, LANES), 1)
    sub = lax.broadcasted_iota(jnp.int32, (TILE, LANES), 0)
    logs = jnp.zeros((1, LANES), F32)
    width = 2 * SUBS
    for g in range(LANES // width):
        panel = list(tiles[4 * g : 4 * g + 4])
        for s in range(2):
            p = 2 * g + s
            cur, dets, inside = solve16(panel[2 * s : 2 * s + 2], p, lane, sub)
            for m in range(0, len(dets), 4):
                quad = (dets[m] * dets[m + 1]) * (dets[m + 2] * dets[m + 3])
                logs = logs + jnp.log(quad)
            spread = [rows8(cur[m // TILE], m % TILE) for m in range(SUBS)]
            new = list(panel)
            for i in range(4):
                if i // 2 == s:
                    new[i] = cur[i % 2]
                    continue
                parts = [lane8(panel[i], SUBS * p + m) * spread[m] for m in range(SUBS)]
                while len(parts) > 1:
                    parts = [parts[m] + parts[m + 1] for m in range(0, len(parts), 2)]
                new[i] = jnp.where(inside, 0.0, panel[i]) - parts[0]
            panel = new
        high, low = split(jnp.concatenate(panel, 0))
        left = split(jnp.concatenate(tiles, 0))

        def padded(v):
            parts = [v]
            if g:
                parts.insert(0, jnp.zeros((width * g, LANES), BF16))
            if width * (g + 1) < LANES:
                parts.append(jnp.zeros((LANES - width * (g + 1), LANES), BF16))
            return jnp.concatenate(parts, 0)

        right = padded(high)
        update = nn(jnp.concatenate(left, 1), jnp.concatenate([right, right], 0))
        update = update + nn(left[0], padded(low))
        inside = (lane >= width * g) & (lane < width * (g + 1))
        tiles = [
            panel[i - 4 * g]
            if 4 * g <= i < 4 * g + 4
            else jnp.where(inside, 0.0, tiles[i]) - update[TILE * i : TILE * i + TILE]
            for i in range(LANES // TILE)
        ]
    return tiles, logs


CHUNK = 256
HALF = 384
NODES = 2 * HALF
FIX = 32
PARTS = HALF // LANES


def nt(a, b):
    return lax.dot_general(a, b, (((1,), (1,)), ((), ())), preferred_element_type=F32)


def nt3(a, b):
    return nt(a[0], b[0]) + (nt(a[0], b[1]) + nt(a[1], b[0]))


def diag_slot(r, s):
    return r * (r + 1) // 2 + s


def off_slot(r, s):
    return 6 + s * (s + 1) // 2 + r


def blk(r):
    return slice(r * LANES, r * LANES + LANES)


def pack(dst, value):
    for r in range(PARTS):
        for s in range(PARTS):
            if r >= s:
                dst[diag_slot(r, s)] = value[blk(r), blk(s)]
            if r <= s:
                dst[off_slot(r, s)] = value[blk(r), HALF + s * LANES : HALF + (s + 1) * LANES]


def unpack_block(mine, theirs, r, s):
    if s < PARTS:
        return mine(diag_slot(r, s)) if r >= s else mine(diag_slot(s, r)).T
    s -= PARTS
    return mine(off_slot(r, s)) if r <= s else theirs(off_slot(s, r)).T


def eliminate(o_ref, hi_ref, lo_ref, l_ref, col, top, low, u_ref, d_ref):
    size = o_ref.shape[0]
    count = size // LANES
    col[...] = jnp.zeros(col.shape, BF16)
    top[...] = jnp.zeros(top.shape, BF16)
    low[...] = jnp.zeros(low.shape, BF16)
    u_ref[...] = o_ref[0:LANES, :]
    d_ref[...] = o_ref[0:LANES, 0:LANES]

    def late_update():
        for n in range(0, size, CHUNK):
            cs = slice(n, n + CHUNK)
            update = nn(col[...], top[:, cs]) + nn(col[:, 0:LANES], low[:, cs])
            o_ref[:, cs] = o_ref[:, cs] - update

    def at(k):
        return pl.ds(pl.multiple_of(k * LANES, LANES), LANES)

    def body(k, logs):
        ks, before, after = at(k), at(jnp.maximum(k - 1, 0)), at(jnp.minimum(k + 1, count - 1))
        late_update()
        tiles, more = invert128([d_ref[TILE * i : TILE * i + TILE, :] for i in range(LANES // TILE)])
        o_ref[before, :] = u_ref[...]
        block = jnp.concatenate(tiles, 0)
        parts = split(block)
        wide = jnp.concatenate(parts, 1)

        def solve(right):
            return nn(wide, jnp.concatenate([right[0], right[0]], 0)) + nn(parts[0], right[1])

        high, rest = split(o_ref[:, ks])
        col[:, 0:LANES] = high
        col[:, LANES : 2 * LANES] = rest
        ahead = split(solve(split(o_ref[ks, after])))
        left = col[after, :]
        update = nn(left, jnp.concatenate([ahead[0], ahead[0]], 0)) + nn(left[:, 0:LANES], ahead[1])
        d_ref[...] = o_ref[after, after] - update
        u_ref[...] = solve(split(o_ref[ks, :]))
        u_ref[:, ks] = block
        high, rest = split(u_ref[...])
        top[0:LANES, :] = high
        top[LANES : 2 * LANES, :] = high
        low[...] = rest
        o_ref[:, ks] = jnp.zeros((size, LANES), F32)
        return logs + more

    logs = lax.fori_loop(0, count, body, jnp.zeros((1, LANES), F32))
    late_update()
    o_ref[size - LANES : size, :] = u_ref[...]
    l_ref[...] = jnp.broadcast_to(logs, (TILE, LANES))
    for r in range(count):
        high, rest = split(o_ref[blk(r), :])
        hi_ref[blk(r), :] = high
        lo_ref[blk(r), :] = rest


def first_inverse_kernel(p_ref, q_ref, po_ref, qo_ref, d_ref, hi_ref, lo_ref, l_ref, m_ref, *more):
    *more, s_ref = more
    s_ref[:HALF, :NODES] = p_ref[...]
    s_ref[:HALF, NODES:] = q_ref[...]
    s_ref[HALF:, :NODES] = po_ref[...]
    s_ref[HALF:, NODES:] = qo_ref[...]
    eye = lax.broadcasted_iota(jnp.int32, (LANES, LANES), 0) == lax.broadcasted_iota(
        jnp.int32, (LANES, LANES), 1
    )
    for n in range(0, NODES, CHUNK):
        m_ref[:, n : n + CHUNK] = nt(s_ref[...], s_ref[n : n + CHUNK, :])
    for r in range(2 * PARTS):
        m_ref[blk(r), blk(r)] += jnp.where(eye, d_ref[0:1, blk(r)], 0.0)
    eliminate(m_ref, hi_ref, lo_ref, l_ref, *more)


def next_inverse_kernel(p_ref, q_ref, po_ref, qo_ref, hi_ref, lo_ref, l_ref, m_ref, *more):
    mine = lambda i: p_ref[i] + q_ref[i]
    theirs = lambda i: po_ref[i] + qo_ref[i]
    for r in range(PARTS):
        for s in range(2 * PARTS):
            block = unpack_block(mine, theirs, r, s)
            m_ref[blk(r), blk(s)] = block
            if s >= PARTS:
                m_ref[blk(s), blk(r)] = block.T
        for s in range(r + 1):
            block = theirs(diag_slot(r, s))
            m_ref[blk(PARTS + r), blk(PARTS + s)] = block
            if s < r:
                m_ref[blk(PARTS + s), blk(PARTS + r)] = block.T
    eliminate(m_ref, hi_ref, lo_ref, l_ref, *more)


class Moves:
    def __init__(self, sems):
        self.sems, self.count, self.open = sems, 0, {}

    def take(self):
        self.count += 1
        return self.sems.at[self.count - 1]

    def copy(self, key, src, dst):
        move = pltpu.make_async_copy(src, dst, self.take())
        move.start()
        self.open[key] = move

    def pick(self, key, flag, a, b, dst):
        sem = self.take()
        first = pltpu.make_async_copy(a, dst, sem)
        second = pltpu.make_async_copy(b, dst, sem)

        @pl.when(flag)
        def _():
            first.start()

        @pl.when(jnp.logical_not(flag))
        def _():
            second.start()

        self.open[key] = first

    def wait(self, *keys):
        for key in keys:
            self.open.pop(key).wait()


def put(xh, xl, at, value):
    rows = value.shape[0]
    high, low = split(value)
    xh[at : at + rows, :] = high
    xl[at : at + rows, :] = low


def put_product(xh, xl, at, a, b):
    rows = slice(at, at + a.shape[0])
    for n in range(0, NODES, CHUNK):
        high, low = split(nt(a[...], b[n : n + CHUNK, :]))
        xh[rows, n : n + CHUNK] = high
        xl[rows, n : n + CHUNK] = low


def turned(x):
    return jnp.concatenate([x[:, HALF:], x[:, :HALF]], axis=1)


def solve_rows(xh, xl, at, rows, hi, lo, ch, cl):
    rs = slice(at, at + rows)
    for n in range(0, NODES, CHUNK):
        cs = slice(n, n + CHUNK)
        high, low = split(dot3((xh[rs, :], xl[rs, :]), (hi[:, cs], lo[:, cs])))
        ch[rs, cs] = high
        cl[rs, cs] = low


def products(ch, cl, at, rows, xh, xl, start, count):
    rs = slice(at, at + rows)
    for n in range(0, count, CHUNK):
        width = min(CHUNK, count - n)
        cs = slice(start + n, start + n + width)
        yield slice(n, n + width), nt3((ch[rs, :], cl[rs, :]), (xh[cs, :], xl[cs, :]))


def first_w(d, which, k, w):
    eye = lax.broadcasted_iota(jnp.int32, (LANES, LANES), 0) == lax.broadcasted_iota(
        jnp.int32, (LANES, LANES), 1
    )
    for n in range(0, NODES, CHUNK):
        w[:, n : n + CHUNK] = nt(k[0:HALF, :], k[n : n + CHUNK, :])
    for r in range(PARTS):
        w[blk(r), blk(r)] += jnp.where(eye, d[which : which + 1, blk(r)], 0.0)


def factor_moves(moves, key, flag, which, f, names, dst):
    n = f[names[0]].shape[0]
    for side in range(2):
        pair = [f[name + "o" * side] for name in names]
        a, b = pair if which == 0 else pair[::-1]
        moves.pick(key + "ab"[side], flag, a, b, dst.at[side * n : side * n + n])


def coupling_moves(moves, key, flag, which, f, dst):
    for side in range(2):
        pair = [f[name + "o" * side].at[0:HALF] for name in "xy"]
        a, b = pair if which == 0 else pair[::-1]
        moves.pick(key + "ab"[side], flag, a, b, dst.at[side * HALF : side * HALF + HALF])


def put_coupling(moves, key, buf, which, xh, xl):
    moves.wait(key + "a")
    for r in range(PARTS):
        put(xh, xl, which * NODES + r * LANES, buf[blk(r), :])
    moves.wait(key + "b")
    for r in range(PARTS):
        value = buf[HALF + r * LANES : HALF + (r + 1) * LANES, :]
        put(xh, xl, which * NODES + HALF + r * LANES, turned(value))


def put_small(buf, xh, xl, wk, flag):
    at = slice(0, FIX)
    put(xh, xl, 2 * NODES, jnp.concatenate(
        [buf[0, at, :] + buf[1, at, :], turned(buf[2, at, :] + buf[3, at, :])], axis=0
    ))
    at = slice(FIX, 2 * FIX)
    own, got = buf[0, at, :], buf[1, at, :]
    wk[0:FIX, 0:NODES] = jnp.where(flag, own, got)
    wk[0:FIX, NODES : 2 * NODES] = jnp.where(flag, got, own)
    at = slice(2 * FIX, 3 * FIX)
    wk[0:FIX, 2 * NODES : 2 * NODES + LANES] = buf[0, at, 0:LANES] + buf[1, at, 0:LANES]


def small_moves(moves, f, buf):
    for i, name in enumerate(("x", "y", "xo", "yo")):
        moves.copy("s%d" % i, f[name].at[HALF : HALF + 3 * FIX], buf.at[i])


def unpack_rows(v, vo, w):
    for r in range(PARTS):
        for s in range(2 * PARTS):
            w[blk(r), blk(s)] = unpack_block(lambda i: v[i], lambda i: vo[i], r, s)


def joined_logs(buf, l_ref):
    logs = jnp.broadcast_to(l_ref[0:1, :], (FIX, LANES))
    if buf is not None:
        at = slice(2 * FIX, 3 * FIX)
        logs = logs + (buf[0, at, LANES : 2 * LANES] + buf[1, at, LANES : 2 * LANES])
    return logs


def pivot_first_kernel(names, flag_ref, hi_any, lo_any, *refs):
    f = dict(zip(names, refs))
    out, sems, hi, lo, xh, xl, ch, cl, w1, p, k, d = refs[len(names) :]
    flag = flag_ref[0] == 1
    moves = Moves(sems)
    factor_moves(moves, "k", flag, 0, f, "kj", k)
    factor_moves(moves, "p", flag, 0, f, "pq", p)
    moves.copy("d", f["d"], d)
    moves.copy("hi", hi_any, hi)
    moves.copy("lo", lo_any, lo)
    moves.wait("ka", "kb", "pa", "pb")
    put_product(xh, xl, 0, k, p)
    moves.wait("d")
    first_w(d, 0, k, w1)
    moves.wait("hi", "lo")
    solve_rows(xh, xl, 0, HALF, hi, lo, ch, cl)
    for cs, value in products(ch, cl, 0, HALF, xh, xl, 0, NODES):
        w1[:, cs] = w1[:, cs] - value
    pack(out, w1)


def pivot_next_kernel(names, flag_ref, hi_any, lo_any, *refs):
    f = dict(zip(names, refs))
    out, sems, hi, lo, xh, xl, ch, cl, w1, x = refs[len(names) :]
    flag = flag_ref[0] == 1
    moves = Moves(sems)
    coupling_moves(moves, "x", flag, 0, f, x)
    moves.copy("hi", hi_any, hi)
    moves.copy("lo", lo_any, lo)
    moves.copy("w", f["w"], w1)
    put_coupling(moves, "x", x, 0, xh, xl)
    moves.wait("hi", "lo")
    solve_rows(xh, xl, 0, HALF, hi, lo, ch, cl)
    moves.wait("w")
    for cs, value in products(ch, cl, 0, HALF, xh, xl, 0, NODES):
        w1[:, cs] = jnp.where(flag, w1[:, cs], 0.0) - value
    pack(out, w1)


def rest_tail(hi, lo, xh, xl, ch, cl, w2, wk, cpl, rr, packed, logs):
    solve_rows(xh, xl, NODES, HALF, hi, lo, ch, cl)
    solve_rows(xh, xl, 2 * NODES, FIX, hi, lo, ch, cl)
    for cs, value in products(ch, cl, NODES, HALF, xh, xl, 0, NODES):
        cpl[0:HALF, cs] = -value
    for cs, value in products(ch, cl, NODES, HALF, xh, xl, NODES, NODES):
        rr[:, cs] = w2[:, cs] - value
    at = 2 * NODES
    for s in range(2):
        rows = slice(HALF + s * FIX, HALF + (s + 1) * FIX)
        cpl[rows, :] = wk[:, s * NODES : (s + 1) * NODES]
        for cs, value in products(ch, cl, at, FIX, xh, xl, s * NODES, NODES):
            cpl[rows, cs] = cpl[rows, cs] - value
    last = slice(HALF + 2 * FIX, HALF + 3 * FIX)
    cpl[last, :] = jnp.zeros((FIX, NODES), F32)
    for cs, value in products(ch, cl, at, FIX, xh, xl, at, 2 * FIX):
        cpl[last, cs] = wk[:, at : at + 2 * FIX] - value
    cpl[last, LANES : 2 * LANES] = logs
    pack(packed, rr)


def rest_first_kernel(names, flag_ref, hi_any, lo_any, l_ref, *refs):
    f = dict(zip(names, refs))
    cpl, rr, packed, sems, hi, lo, xh, xl, ch, cl, w2, wk, p, k, p2, k2, e, g, d = refs[len(names) :]
    flag = flag_ref[0] == 1
    moves = Moves(sems)
    factor_moves(moves, "p", flag, 0, f, "pq", p)
    factor_moves(moves, "k", flag, 0, f, "kj", k)
    factor_moves(moves, "e", flag, 0, f, "eg", e)
    factor_moves(moves, "g", flag, 1, f, "eg", g)
    factor_moves(moves, "P", flag, 1, f, "pq", p2)
    factor_moves(moves, "K", flag, 1, f, "kj", k2)
    moves.copy("d", f["d"], d)
    moves.copy("hi", hi_any, hi)
    moves.copy("lo", lo_any, lo)
    moves.wait("pa", "pb", "ka", "kb", "ea", "eb", "ga", "gb")
    put_product(xh, xl, 0, k, p)
    wk[0:FIX, 0:NODES] = nt(e[0:FIX, :], k[...])
    wk[0:FIX, 2 * NODES : 2 * NODES + 2 * FIX] = nt(e[0:FIX, :], e[...]) + nt(g[0:FIX, :], g[...])
    moves.wait("Pa", "Pb", "Ka", "Kb")
    put(xh, xl, 2 * NODES, nt(e[...], p[...]) + nt(g[...], p2[...]))
    wk[0:FIX, NODES : 2 * NODES] = nt(g[0:FIX, :], k2[...])
    put_product(xh, xl, NODES, k2, p2)
    moves.wait("d")
    first_w(d, 1, k2, w2)
    moves.wait("hi", "lo")
    rest_tail(hi, lo, xh, xl, ch, cl, w2, wk, cpl, rr, packed, joined_logs(None, l_ref))


def rest_next_kernel(names, flag_ref, hi_any, lo_any, l_ref, *refs):
    f = dict(zip(names, refs))
    cpl, rr, packed, sems, hi, lo, xh, xl, ch, cl, w2, wk, x, z, small, v, vo = refs[len(names) :]
    flag = flag_ref[0] == 1
    moves = Moves(sems)
    coupling_moves(moves, "z", flag, 1, f, z)
    small_moves(moves, f, small)
    moves.copy("hi", hi_any, hi)
    moves.copy("lo", lo_any, lo)
    coupling_moves(moves, "x", flag, 0, f, x)
    moves.copy("w", f["w"], w2)
    moves.copy("v", f["v"], v)
    moves.copy("vo", f["vo"], vo)
    put_coupling(moves, "z", z, 1, xh, xl)
    moves.wait("s0", "s1", "s2", "s3")
    put_small(small, xh, xl, wk, flag)
    put_coupling(moves, "x", x, 0, xh, xl)
    moves.wait("hi", "lo", "w", "v", "vo")

    @pl.when(flag)
    def _():
        unpack_rows(v, vo, w2)

    rest_tail(hi, lo, xh, xl, ch, cl, w2, wk, cpl, rr, packed, joined_logs(small, l_ref))


def halves(core, b):
    return [pl.multiple_of(side * HALF + b * NODES, LANES) for side in (core, 1 - core)]


def final_kernel(names, flag_ref, hi_any, lo_any, l_ref, *refs):
    f = dict(zip(names, refs))
    ends, part, arrow, logs, sems, outs, hi, lo, xh, xl, ch, cl, w, wk, x, z, small, *bufs = refs[
        len(names) :
    ]
    flag = flag_ref[0] == 1
    core = flag_ref[1]
    moves = Moves(sems)
    coupling_moves(moves, "x", flag, 0, f, x)
    moves.copy("hi", hi_any, hi)
    moves.copy("lo", lo_any, lo)
    coupling_moves(moves, "z", flag, 1, f, z)
    small_moves(moves, f, small)
    moves.copy("w", f["w"], w)
    put_coupling(moves, "x", x, 0, xh, xl)
    moves.wait("hi", "lo")
    solve_rows(xh, xl, 0, HALF, hi, lo, ch, cl)
    put_coupling(moves, "z", z, 1, xh, xl)
    solve_rows(xh, xl, NODES, HALF, hi, lo, ch, cl)
    moves.wait("w", "s0", "s1", "s2", "s3")
    put_small(small, xh, xl, wk, flag)
    solve_rows(xh, xl, 2 * NODES, FIX, hi, lo, ch, cl)
    waits = []
    for i, (b, s) in enumerate(((0, 0), (1, 1), (0, 1), (1, 0))):
        buf = bufs[i]
        for cs, value in products(ch, cl, b * NODES, HALF, xh, xl, s * NODES, NODES):
            buf[:, cs] = -value
        sources = [buf.at[:, 0:HALF], buf.at[:, HALF:NODES]]
        places = [ends.at[b, :, pl.ds(at, HALF)] for at in halves(core, s)]
        out = [pltpu.make_async_copy(sources[h], places[h], outs.at[2 * i + h]) for h in range(2)]
        waits += out
        if b != s:
            for move in out:
                move.start()
            continue
        native = flag if b == 0 else jnp.logical_not(flag)

        @pl.when(native)
        def _():
            buf[...] = buf[...] + w[...]
            for move in out:
                move.start()

        @pl.when(jnp.logical_not(native))
        def _():
            for h in range(2):
                pltpu.make_async_copy(
                    sources[h], part.at[:, h * HALF : (h + 1) * HALF], outs.at[2 * i + h]
                ).start()

    at = 2 * NODES
    for s in range(2):
        own, far = halves(core, s)
        for cs, value in products(ch, cl, at, FIX, xh, xl, s * NODES, NODES):
            wk[:, slice(s * NODES + cs.start, s * NODES + cs.stop)] -= value
        arrow[:, pl.ds(own, HALF)] = wk[:, s * NODES : s * NODES + HALF]
        arrow[:, pl.ds(far, HALF)] = wk[:, s * NODES + HALF : (s + 1) * NODES]
    ((cs, value),) = products(ch, cl, at, FIX, xh, xl, at, 2 * FIX)
    value = wk[:, at : at + 2 * FIX] - value
    swapped = jnp.concatenate([value[:, FIX:], value[:, :FIX]], axis=1)
    arrow[:, at : at + 2 * FIX] = jnp.where(core == 0, value, swapped)
    logs[0] = jnp.sum(joined_logs(small, l_ref)[0:1, 0:1]) * (1.0 / (7 * NODES))
    for move in waits:
        move.wait()


def finish_kernel(flag_ref, ends_in, part, v, vo, ends, outs, buf):
    core = flag_ref[1]
    block = flag_ref[0]
    unpack_rows(v, vo, buf)
    buf[...] = buf[...] + part[...]
    moves = []
    for h, side in enumerate((core, 1 - core)):
        at = pl.multiple_of(side * HALF + block * NODES, LANES)
        moves.append(
            pltpu.make_async_copy(
                buf.at[:, h * HALF : (h + 1) * HALF],
                ends.at[block, :, pl.ds(at, HALF)],
                outs.at[h],
            )
        )
        moves[-1].start()
    for move in moves:
        move.wait()


SMEM = pl.BlockSpec(memory_space=pltpu.SMEM)
VMEM = pl.BlockSpec(memory_space=pltpu.VMEM)


def shape(*dims, dtype=F32):
    return jax.ShapeDtypeStruct(dims, dtype)


ANY = pl.BlockSpec(memory_space=pl.ANY)


def launch(kernel, name, flops, out, scratch, args, scalars=None, specs=None, out_specs=None, alias=None):
    specs = specs or [VMEM] * len(args)
    if scalars is not None:
        specs, args = [SMEM] + specs, [scalars] + list(args)
    return pl.pallas_call(
        kernel,
        out_shape=out,
        in_specs=specs,
        out_specs=out_specs or jax.tree.map(lambda _: VMEM, out),
        scratch_shapes=[
            pltpu.VMEM(s.shape, s.dtype) if isinstance(s, jax.ShapeDtypeStruct) else s
            for s in scratch
        ],
        compiler_params=pltpu.CompilerParams(vmem_limit_bytes=(60 if scalars is None else 50) << 20),
        cost_estimate=pl.CostEstimate(
            flops=flops, bytes_accessed=8 << 20, transcendentals=NODES
        ),
        input_output_aliases=alias or {},
        name=name,
    )(*args)


PACKED = shape(12, LANES, LANES)
SQUARE = shape(NODES, NODES)
SQUARE16 = shape(NODES, NODES, dtype=BF16)
ROWS = shape(HALF, NODES)
STACK16 = shape(2 * (NODES + FIX), NODES, dtype=BF16)
WIDE = shape(FIX, 2 * NODES + LANES)
SEMS = pltpu.SemaphoreType.DMA((24,))
X_ROWS = shape(NODES, NODES)
SMALL = shape(4, 3 * FIX, NODES)
DIAG = shape(2, HALF)
BOTH16 = (SQUARE16, SQUARE16)
STACKS = (SEMS,) + BOTH16 + (STACK16,) * 4
EFF16 = shape(2 * FIX, NODES, dtype=BF16)
INV_SCRATCH = (
    SQUARE,
    shape(NODES, 2 * LANES, dtype=BF16),
    shape(2 * LANES, NODES, dtype=BF16),
    shape(LANES, NODES, dtype=BF16),
    shape(LANES, NODES),
    shape(LANES, LANES),
)
INV_OUT = (SQUARE16, SQUARE16, shape(TILE, LANES))


def shards(spatial, transition, effect, diag):
    steps = lax.axis_size("tm")
    index = lax.axis_index("tm")
    core = lax.axis_index("blk")
    bit = [(index // 2**r) % 2 for r in range(3)]

    def other(x):
        return lax.ppermute(x, "blk", [(0, 1), (1, 0)])

    def partner(x, level):
        if level == 1:
            pairs = [(t, (t // 4) * 4 + 3 - t % 4) for t in range(steps)]
        else:
            pairs = [(t, t ^ (1, 2, 4)[level]) for t in range(steps)]
        return lax.ppermute(x, "tm", pairs)

    def scalars(flag):
        return jnp.stack([flag.astype(jnp.int32), core.astype(jnp.int32)])

    lower = bit[0] == 0
    f = {}
    diag_got = partner(diag, 0)
    f["p"] = jnp.where(lower, transition, spatial)
    f["q"] = partner(f["p"], 0)
    f["po"] = other(f["p"])
    pivot_diag = jnp.where(lower, diag_got, diag)
    pivot_diag = jnp.concatenate([pivot_diag, other(pivot_diag)])[None]
    keep_diag = jnp.where(lower, diag, diag_got)
    after = bit[1] == 1
    f["d"] = jnp.stack([jnp.where(after, keep_diag, 0.0), jnp.where(after, 0.0, keep_diag)])
    keep = jnp.where(lower, spatial, transition)
    all_flags = [
        scalars(flag) for flag in (bit[0] != bit[1], bit[1] != bit[2], bit[2] == 0)
    ]
    f["q"], f["d"], pivot_diag, keep, effect, all_flags = lax.optimization_barrier(
        (f["q"], f["d"], pivot_diag, keep, effect, all_flags)
    )
    f["qo"] = other(f["q"])
    f["k"] = keep
    f["j"] = partner(keep, 0)
    f["e"] = effect
    f["g"] = partner(effect, 0)
    hi, lo, logs = launch(
        first_inverse_kernel,
        "first_inverse",
        30_000_000_000,
        INV_OUT,
        INV_SCRATCH + (shape(NODES, 2 * NODES, dtype=BF16),),
        [f["p"], f["q"], f["po"], f["qo"], pivot_diag],
    )
    f["ko"], f["eo"] = other(f["k"]), other(f["e"])
    f["j"], f["g"], logs = lax.optimization_barrier((f["j"], f["g"], logs))
    f["jo"], f["go"] = other(f["j"]), other(f["g"])
    flags = all_flags[0]
    for level in (1, 2):
        names = [n for n in f]
        args = [f[n] for n in names]
        first = level == 1
        piece = launch(
            functools.partial(pivot_first_kernel if first else pivot_next_kernel, names),
            "pivot%d" % level,
            5_000_000_000,
            PACKED,
            STACKS + (ROWS,) + (BOTH16 + (DIAG,) if first else (X_ROWS,)),
            [hi, lo] + args,
            flags,
            [ANY] * (2 + len(args)),
        )
        if not first:
            packed_got, piece = lax.optimization_barrier((packed_got, piece))
            piece = piece + jnp.where(flags[0] == 1, 0.0, packed_got)
            f["v"] = packed_got
            f["vo"] = other(packed_got)
            names, args = names + ["v", "vo"], args + [f["v"], f["vo"]]
        piece_got = partner(piece, level)
        piece_other = other(piece)
        cpl, rr, packed = launch(
            functools.partial(rest_first_kernel if first else rest_next_kernel, names),
            "rest%d" % level,
            9_000_000_000,
            (shape(HALF + 3 * FIX, NODES), ROWS, PACKED),
            STACKS
            + (ROWS, WIDE)
            + (BOTH16 * 2 + (EFF16, EFF16, DIAG) if first else (X_ROWS, X_ROWS, SMALL, PACKED, PACKED)),
            [hi, lo, logs] + args,
            flags,
            [ANY, ANY, VMEM] + [ANY] * len(args),
        )
        piece_got, cpl = lax.optimization_barrier((piece_got, cpl))
        piece_got_other = other(piece_got)
        f = {"x": cpl, "y": partner(cpl, level), "xo": other(cpl), "w": rr}
        hi, lo, logs = launch(
            next_inverse_kernel,
            "inverse%d" % level,
            30_000_000_000,
            INV_OUT,
            INV_SCRATCH,
            [piece, piece_got, piece_other, piece_got_other],
        )
        f["y"], packed, logs = lax.optimization_barrier((f["y"], packed, logs))
        packed_got = partner(packed, level)
        f["yo"] = other(f["y"])
        flags = all_flags[level]
    names = [n for n in f]
    ends, part, arrow, logs = launch(
        functools.partial(final_kernel, names),
        "final",
        20_000_000_000,
        (shape(2, HALF, 2 * NODES), ROWS, shape(FIX, 2 * (NODES + FIX)), shape(1)),
        (SEMS, pltpu.SemaphoreType.DMA((8,))) + STACKS[1:] + (ROWS, WIDE, X_ROWS, X_ROWS, SMALL) + (ROWS,) * 4,
        [hi, lo, logs] + [f[n] for n in names],
        flags,
        [ANY, ANY, VMEM] + [ANY] * len(names),
        (ANY, ANY, VMEM, SMEM),
    )
    packed_got, part = lax.optimization_barrier((packed_got, part))
    ends = launch(
        finish_kernel,
        "finish",
        1_000_000_000,
        shape(2, HALF, 2 * NODES),
        (pltpu.SemaphoreType.DMA((2,)), ROWS),
        [ends, part, packed_got, other(packed_got)],
        flags,
        [ANY, VMEM, VMEM, VMEM],
        ANY,
        {1: 0},
    )
    return ends[None], arrow[None], logs


def solution(mesh):
    return jax.shard_map(
        shards,
        mesh=mesh,
        in_specs=(
            P(("tm", "blk"), None),
            P(("tm", "blk"), None),
            P(("tm", "blk"), None),
            P(("tm", "blk")),
        ),
        out_specs=(P("tm", None, "blk", None), P("tm", "blk", None), P("tm")),
        check_vma=False,
    )
```
